256 devices in a mesh: rows: 8 (over x, core), cols: 32 (over y, z).
Axes of the slice: x: 4, y: 4, z: 8, core: 2. Of those that a mesh axis runs over, the one named last changes fastest.
Arguments:
- forcing: float32 [32, 2, 512, 8192], P(None, None, 'cols', 'rows'), may hold values from -3 to 3
- material: int32 [2, 512, 8192], P(None, 'cols', 'rows'), may hold values from 0 to 7
- capacity_table: float32 [8], replicated, may hold values from 0.5 to 2
- conductance_table: float32 [8], replicated, may hold values from 0.25 to 2
- sink_table: float32 [8], replicated, may hold values from 0.1 to 1
Outputs:
- initial_sensitivity: float32 [2, 512, 8192], P(None, 'cols', 'rows')
- window_mean: float32 [2, 512, 8192], P(None, 'cols', 'rows')
- residual_norms: float32 [3], replicated
The draws below stay inside these ranges and needn't reach their ends.
All inputs are finite; a program needn't handle non-finite values.
Results may differ from the reference program's by a relative error of at most 0.0001.
Values sent between devices are 32-bit elements; how exact they have to be, the bound alone decides.
No kernel may reach another device: no remote copies, remote signals or barrier semaphores. Data moves between devices by JAX's collectives and lax.ppermute only.
A program may use at most 128 MiB of HBM per device.

```python
import math
import jax
import jax.numpy as jnp
from jax import lax

CC = 16
CR = 1024
STEPS = 32
PASSES = 8
SWEEPS = 3
MATERIALS = 8
NC = 512
NR = 8192


def plant(array, rng, low, high):
    dims = array.shape
    index_at = [jax.random.randint(jax.random.fold_in(rng, axis), (), 0, dims[axis]) for axis in range(len(dims))]
    array = array.at[tuple(index_at)].set(low)
    longest = dims.index(max(dims))
    index_at[longest] = (index_at[longest] + 1) % dims[longest]
    return array.at[tuple(index_at)].set(high)


def block_scale(rng, extent, pieces, smallest, largest):
    factor_of = 1.0
    for axis_at, shards_of in pieces:
        steps = jax.random.uniform(jax.random.fold_in(jax.random.fold_in(rng, 6), axis_at), (shards_of,), jnp.float32, smallest / len(pieces), largest / len(pieces))
        factor_of = factor_of * jnp.repeat(jnp.exp(steps), extent[axis_at] // shards_of).reshape((-1,) + (1,) * (len(extent) - 1 - axis_at))
    return factor_of


def noise(own_key, dims, deviation, most, cuts=(), kind=jnp.bfloat16):
    result = deviation * jax.random.normal(own_key, dims, jnp.float32)
    if cuts:
        result = result * block_scale(own_key, dims, cuts, -0.22, 0.18)
    return jnp.clip(result, -most, most).astype(kind)


def setup_inputs(seed: int = 0) -> dict:
    splits = jax.random.split(jax.random.key(seed), 6)
    return {
        "forcing": noise(splits[0], (STEPS, 2, NC, NR), 0.5, 3.0, ((2, 32), (3, 8)), jnp.float32),
        "material": plant(jax.random.randint(splits[1], (2, NC, NR), 0, MATERIALS), jax.random.fold_in(splits[1], 1), 0, MATERIALS - 1).astype(jnp.int32),
        "capacity_table": jnp.clip(jnp.exp(jax.random.uniform(splits[2], (MATERIALS,), jnp.float32, math.log(0.5), math.log(2.0))), 0.5, 2.0),
        "conductance_table": jnp.clip(jnp.exp(jax.random.uniform(splits[3], (MATERIALS,), jnp.float32, math.log(0.25), math.log(2.0))), 0.25, 2.0),
        "sink_table": jnp.clip(jnp.exp(jax.random.uniform(splits[4], (MATERIALS,), jnp.float32, math.log(0.1), math.log(1.0))), 0.1, 1.0),
    }


def shifted(field, axis, offset):
    length = field.shape[axis]
    widths = [(0, 0)] * field.ndim
    if offset > 0:
        kept = lax.slice_in_dim(field, 1, length, axis=axis)
        widths[axis] = (0, 1)
    else:
        kept = lax.slice_in_dim(field, 0, length - 1, axis=axis)
        widths[axis] = (1, 0)
    return jnp.pad(kept, widths)

def couple(conduct, other):
    return 2.0 * conduct * other / (conduct + other)

def cross_sum(field, outer):
    total = outer[0] * shifted(field, 1, 1) + outer[1] * shifted(field, 1, -1)
    return total + outer[2] * shifted(field, 2, 1) + outer[3] * shifted(field, 2, -1)

def neighbour_sum(field, inner, vertical):
    total = inner[0] * shifted(field, 1, 1) + inner[1] * shifted(field, 1, -1)
    total = total + inner[2] * shifted(field, 2, 1) + inner[3] * shifted(field, 2, -1)
    return total + vertical * field[::-1]

def reference(forcing, material, capacity_table, conductance_table, sink_table):
    capacity = capacity_table[material]
    conduct = conductance_table[material]
    sink = sink_table[material]
    directions = [(1, 1), (1, -1), (2, 1), (2, -1)]
    edges = [couple(conduct, shifted(conduct, axis, offset)) for axis, offset in directions]
    vertical = couple(conduct, conduct[::-1])
    diagonal = capacity + sink + edges[0] + edges[1] + edges[2] + edges[3] + vertical
    column = jnp.arange(NC, dtype=jnp.int32)
    row = jnp.arange(NR, dtype=jnp.int32)
    masks = [(column % CC != CC - 1)[None, :, None], (column % CC != 0)[None, :, None], (row % CR != CR - 1)[None, None, :], (row % CR != 0)[None, None, :]]
    inner = [jnp.where(mask, edge, 0.0) for mask, edge in zip(masks, edges)]
    outer = [jnp.where(mask, 0.0, edge) for mask, edge in zip(masks, edges)]
    profile = jnp.power(jnp.float32(3.0), column.astype(jnp.float32)[:, None] / float(NC) + row.astype(jnp.float32)[None, :] / float(NR))
    count = float(STEPS * 2 * NC * NR)

    def advance(later, inputs):
        force_now, prev_now = inputs
        rhs = force_now * profile + capacity * later + cross_sum(prev_now, outer)
        field = later
        for turn in range(PASSES):
            field = (rhs + neighbour_sum(field, inner, vertical)) / diagonal
        return (field, field)
    previous = jnp.zeros_like(forcing)
    norms = []
    first = jnp.zeros(forcing.shape[1:], jnp.float32)
    wave = previous
    for sweep in range(SWEEPS):
        first, wave = lax.scan(advance, jnp.zeros(forcing.shape[1:], jnp.float32), (forcing, previous), reverse=True)
        change = wave - previous
        norms.append(jnp.sqrt(jnp.sum(change * change) / count + 1e-06))
        previous = wave
    initial_sensitivity = capacity * first
    window_mean = lax.optimization_barrier(jnp.sum(wave, 0)) / STEPS
    return (initial_sensitivity, window_mean, jnp.stack(norms))
```

```python
import functools
import math

import jax
import jax.numpy as jnp
from jax import lax
from jax.experimental import pallas as pl
from jax.experimental.pallas import tpu as pltpu
from jax.sharding import PartitionSpec as P

PASSES = 8
SWEEPS = 3
F32 = jnp.float32
BF16 = jnp.bfloat16
VMEM_LIMIT = 56 * 2**20

CELLS = [(a, h, j) for a in range(2) for h in range(2) for j in range(8)]
GHOSTS = [(a, h, j) for a in range(2) for h in range(2) for j in (-1, 8)]
WIDE = CELLS + GHOSTS
CP, CM, RP, RM, VV = range(5)


def home(p):
    return (p[0], p[1], p[2] % 8)


def colour(p):
    return sum(p) % 2


UNIT = set()
for _a in range(2):
    for _h in range(2):
        for _j in range(8):
            if _j > 3:
                UNIT.add((RM, (_a, _h, _j)))
            if _j < 3:
                UNIT.add((RP, (_a, _h, _j)))
    UNIT.add((CM, (_a, 1, 3)))
UNIT.add((VV, (1, 0, 3)))

AT = {p: i for i, p in enumerate(WIDE)}
KEYS = [("w", d, p) for p in WIDE for d in range(5) if (d, home(p)) not in UNIT]
KEYS += [("e", 0, p) for p in WIDE]
KEYS += [("alpha", 0, p) for p in CELLS]
KEYS += [("cap", 0, p) for p in CELLS]
KEYS += [("g", 0, p) for p in CELLS]
KEYS += [("oc", side, a) for side in range(2) for a in range(2)]
KEYS += [("or", side, q) for side in range(2) for q in range(4)]
COEF = {k: i for i, k in enumerate(KEYS)}


def lanes():
    return lax.broadcasted_iota(jnp.int32, (8, 128), 1)


def sublanes():
    return lax.broadcasted_iota(jnp.int32, (8, 128), 0)


def neighbour(x, p, d, cache):
    a, h, j = p

    def turned(source, shift):
        key = (source, shift)
        if key not in cache:
            cache[key] = pltpu.roll(x[source], shift, 0)
        return cache[key]

    if d == VV:
        return x[(1 - a, h, j)]
    if d == CP:
        return x[(a, 1, j)] if h == 0 else turned((a, 0, j), 7)
    if d == CM:
        return x[(a, 0, j)] if h == 1 else turned((a, 1, j), 1)
    return x[(a, h, j + 1)] if d == RP else x[(a, h, j - 1)]


def permutation(to_cells):
    size = 1024
    first = lax.broadcasted_iota(jnp.int32, (size, size), 0)
    second = lax.broadcasted_iota(jnp.int32, (size, size), 1)
    row, place = (first, second) if to_cells else (second, first)
    return jnp.where(row == 8 * (place % 128) + place // 128, 1.0, 0.0).astype(BF16)


def permute_rows(x, matrix):
    high = x.astype(BF16)
    low = (x - high.astype(F32)).astype(BF16)
    return jnp.dot(high, matrix, preferred_element_type=F32) + jnp.dot(low, matrix, preferred_element_type=F32)


def materials_kernel(cap_t, con_t, sink_t, material, cap_o, con_o, sink_o, low_o, high_o, held):
    kinds = material[...].reshape(32, 1024).astype(F32).astype(BF16)
    moved = jnp.dot(kinds, permutation(True), preferred_element_type=F32)
    for j in range(8):
        held[j] = moved[:, j * 128 : (j + 1) * 128]
    for p in CELLS:
        a, h, j = p
        kind = held[j, pl.ds(a * 16 + h, 8, stride=2), :]
        values = [jnp.full((8, 128), t[0], F32) for t in (cap_t, con_t, sink_t)]
        for m in range(1, 8):
            hit = kind > m - 0.5
            values = [jnp.where(hit, t[m], v) for t, v in zip((cap_t, con_t, sink_t), values)]
        i = AT[p]
        cap_o[i], con_o[pl.ds(i * 8, 8), :], sink_o[i] = values
    for a in range(2):
        low_o[a] = con_o[pl.ds(a * 128, 8, stride=8), :]
        high_o[a] = con_o[pl.ds(a * 128 + 64 + 7, 8, stride=8), :]


def forcing_kernel(forcing, out, matrix):
    @pl.when(pl.program_id(0) == 0)
    def _():
        matrix[...] = permutation(True)

    rows = forcing.shape[0] * 32
    moved = permute_rows(forcing[...].reshape(rows, 1024), matrix[...])
    for j in range(8):
        out[j] = moved[:, j * 128 : (j + 1) * 128]


def coefficients(place, sizes, cap, con, sink, con_low, con_high, row_low, row_high, co):
    n_cols, n_rows = sizes
    k = {p: con[pl.ds(AT[p] * 8, 8), :] for p in CELLS}
    edge_in = {}
    edge_out = {}
    lane, sub = lanes(), sublanes()

    def couple(x, y):
        return 2.0 * x * y / (x + y)

    weight = {}
    inverse = {}
    for p in CELLS:
        a, h, j = p
        q = a * 2 + h
        others = []
        if h == 0:
            others.append((k[(a, 1, j)], None))
            left = jnp.broadcast_to(con_low[a, pl.ds(j, 1), :], (8, 128))
            others.append((jnp.where(sub == 0, left, pltpu.roll(k[(a, 1, j)], 1, 0)), sub == 0))
        else:
            right = jnp.broadcast_to(con_high[a, pl.ds(j, 1), :], (8, 128))
            others.append((jnp.where(sub == 7, right, pltpu.roll(k[(a, 0, j)], 7, 0)), sub == 7))
            others.append((k[(a, 0, j)], None))
        if j < 7:
            others.append((k[(a, h, j + 1)], None))
        else:
            after = jnp.where(lane == 127, pltpu.roll(row_high[q], 127, 1), pltpu.roll(k[(a, h, 0)], 127, 1))
            others.append((after, lane == 127))
        if j > 0:
            others.append((k[(a, h, j - 1)], None))
        else:
            before = jnp.where(lane == 0, pltpu.roll(row_low[q], 1, 1), pltpu.roll(k[(a, h, 7)], 1, 1))
            others.append((before, lane == 0))
        others.append((k[(1 - a, h, j)], None))
        edges = [couple(k[p], other) for other, _ in others]
        capacity = cap[AT[p]]
        diagonal = capacity + sink[AT[p]]
        for e in edges:
            diagonal = diagonal + e
        inverse[p] = 1.0 / diagonal
        for d, (e, (_, mask)) in enumerate(zip(edges, others)):
            e = e * inverse[p]
            edge_in[d, p] = e if mask is None else jnp.where(mask, 0.0, e)
            edge_out[d, p] = None if mask is None else jnp.where(mask, e, 0.0)
    alpha = {(0, 0, 3): jnp.ones((8, 128), F32)}
    alpha[(1, 0, 3)] = edge_in[VV, (1, 0, 3)] * alpha[(0, 0, 3)]
    for a in range(2):
        alpha[(a, 1, 3)] = edge_in[CM, (a, 1, 3)] * alpha[(a, 0, 3)]
        for h in range(2):
            for j in range(4, 8):
                alpha[(a, h, j)] = edge_in[RM, (a, h, j)] * alpha[(a, h, j - 1)]
            for j in (2, 1, 0):
                alpha[(a, h, j)] = edge_in[RP, (a, h, j)] * alpha[(a, h, j + 1)]
    for a in range(2):
        for h in range(2):
            alpha[(a, h, -1)] = pltpu.roll(alpha[(a, h, 7)], 1, 1)
            alpha[(a, h, 8)] = pltpu.roll(alpha[(a, h, 0)], 127, 1)

    def put(kind, d, p, value):
        co[COEF[(kind, d, p)]] = value

    cache = {}
    column0 = (place[1] * 16).astype(F32)
    row0 = (place[0] * 1024).astype(F32)
    scaled_out = {}
    for p in CELLS:
        a, h, j = p
        over = 1.0 / alpha[p]
        put("alpha", 0, p, alpha[p])
        put("cap", 0, p, cap[AT[p]] * alpha[p])
        e = cap[AT[p]] * inverse[p] - 1.0
        put("e", 0, p, e)
        column = (2 * sub + h).astype(F32) + column0
        row = (8 * lane + j).astype(F32) + row0
        profile = jnp.exp(math.log(3.0) * (column * (1.0 / n_cols) + row * (1.0 / n_rows)))
        put("g", 0, p, profile * inverse[p] * over)
        if j == 7:
            put("e", 0, (a, h, -1), pltpu.roll(e, 1, 1))
        if j == 0:
            put("e", 0, (a, h, 8), pltpu.roll(e, 127, 1))
        for d in range(5):
            if edge_out[d, p] is not None:
                scaled_out[d, p] = edge_out[d, p] * over
            if (d, p) in UNIT:
                continue
            w = edge_in[d, p] * neighbour(alpha, p, d, cache) * over
            put("w", d, p, w)
            if j == 7:
                put("w", d, (a, h, -1), pltpu.roll(w, 1, 1))
            if j == 0:
                put("w", d, (a, h, 8), pltpu.roll(w, 127, 1))
    for a in range(2):
        low, high = jnp.zeros((8, 128), F32), jnp.zeros((8, 128), F32)
        for j in range(8):
            low = jnp.where(sub == j, jnp.broadcast_to(scaled_out[CM, (a, 0, j)][0:1], (8, 128)), low)
            high = jnp.where(sub == j, jnp.broadcast_to(scaled_out[CP, (a, 1, j)][7:8], (8, 128)), high)
        put("oc", 0, a, low)
        put("oc", 1, a, high)
        for h in range(2):
            put("or", 0, a * 2 + h, scaled_out[RM, (a, h, 0)])
            put("or", 1, a * 2 + h, scaled_out[RP, (a, h, 7)])


def time_step(now, source, extra, co, y, d_ref, t_ref):
    def weight(d, p):
        return co[COEF[("w", d, p)]]

    def load(p):
        return y[pl.ds(AT[p] * 8, 8), :]

    def applied(x, p, cache):
        total = None
        for d in (VV, CP, CM, RP, RM):
            term = neighbour(x, p, d, cache)
            if (d, home(p)) not in UNIT:
                term = weight(d, p) * term
            total = term if total is None else total + term
        return total

    def add_ghosts(x):
        for a, h, j in list(x):
            if j >= 6:
                x[(a, h, j - 8)] = pltpu.roll(x[(a, h, j)], 1, 1)
            if j <= 1:
                x[(a, h, j + 8)] = pltpu.roll(x[(a, h, j)], 127, 1)

    start = [{p: load(p) for p in CELLS if colour(p) == c} for c in range(2)]
    for c in range(2):
        add_ghosts(start[c])
    fields = [dict(start[0]), dict(start[1])]
    done = {}
    for k in range(1, PASSES + 1):
        fresh = [None, None]
        for chain in range(2):
            x = fields[chain]
            to = (chain + k) % 2
            wide = k % 2 == 1
            if wide and k > 1:
                add_ghosts(x)
            cache = {}
            out = {}
            for p in WIDE if wide else CELLS:
                if colour(p) != to:
                    continue
                value = applied(x, p, cache)
                slot = pl.ds(AT[p] * 8, 8)
                if k == 1:
                    base = source(p) + co[COEF[("e", 0, p)]] * start[to][p]
                    if extra is not None and p in extra:
                        base = base + extra[p]
                    value = value + base
                    d_ref[slot, :] = value
                elif k == 5:
                    value = value + d_ref[slot, :]
                    t_ref[slot, :] = value
                elif k == 7:
                    value = value + t_ref[slot, :]
                    d_ref[slot, :] = value
                out[p] = value
            fresh[chain] = out
        fields = fresh
    for p in CELLS:
        slot = pl.ds(AT[p] * 8, 8)
        done[p] = fields[colour(p)][p] + (d_ref[slot, :] + load(p))
    return done


def sweep_kernel(first, last, sizes, *refs):
    refs = list(refs)
    if first:
        (place, cap, con, sink, con_low, con_high, row_low, row_high, forcing) = refs[:9]
        co = refs[9]
        refs = refs[10:]
        coefficients(place, sizes, cap, con, sink, con_low, con_high, row_low, row_high, co)
    else:
        (co, sum_in, final_in, square_in, got_low, got_high, got_row_low, got_row_high) = refs[:8]
        refs = refs[8:]
    if last:
        (start_o, mean_o, square_o, y, d_ref, t_ref, f_ref, sums, squares, held) = refs
    else:
        (sum_o, final_o, square_o, low_o, high_o, row_low_o, row_high_o) = refs[:7]
        (y, d_ref, t_ref, f_ref, sums, squares, rows_ref) = refs[7:]
    steps = 32
    y[...] = jnp.zeros_like(y)
    squares[...] = jnp.zeros_like(squares)
    if first:
        sums[...] = jnp.zeros_like(sums)
    else:
        sums[...] = sum_in[...]
        f_ref[...] = jnp.zeros_like(f_ref)
    if not last:
        rows_ref[...] = jnp.zeros_like(rows_ref)
    lane = lanes()

    def body(i, carry):
        now = steps - 1 - i
        extra = None
        if first:
            memo = {}

            def source(p):
                a, h, j = home(p)
                if (a, h, j) not in memo:
                    rows = pl.ds(now * 32 + a * 16 + h, 8, stride=2)
                    memo[(a, h, j)] = forcing[j, rows, :] * co[COEF[("g", 0, (a, h, j))]]
                value = memo[(a, h, j)]
                if p[2] == -1:
                    value = pltpu.roll(value, 1, 1)
                if p[2] == 8:
                    value = pltpu.roll(value, 127, 1)
                return value

        else:
            extra = {}
            for side, got in enumerate((got_low, got_high)):
                for a in range(2):
                    value = got[now, a] * co[COEF[("oc", side, a)]]
                    base = (a * 2 + side) * 64
                    s = 7 * side
                    f_ref[pl.ds(base + s, 8, stride=8), :] = value
                    f_ref[pl.ds(AT[(a, side, -1)] * 8 + s, 1), :] = pltpu.roll(value, 1, 1)[7:8]
                    f_ref[pl.ds(AT[(a, side, 8)] * 8 + s, 1), :] = pltpu.roll(value, 127, 1)[0:1]
            for q in range(4):
                a, h = q // 2, q % 2
                spot = q * 32 + now
                extra[(a, h, 0)] = co[COEF[("or", 0, q)]] * pltpu.roll(got_row_low[...], (128 - spot) % 128, 1)
                extra[(a, h, 7)] = co[COEF[("or", 1, q)]] * pltpu.roll(got_row_high[...], 127 - spot, 1)

            def source(p):
                return f_ref[pl.ds(AT[p] * 8, 8), :]

        done = time_step(now, source, extra, co, y, d_ref, t_ref)
        for p in CELLS:
            i_p = AT[p]
            x = done[p]
            y[pl.ds(i_p * 8, 8), :] = x
            sums[i_p] += x
            squares[i_p] += x * x
        if not last:
            for a in range(2):
                low_o[now, a] = y[pl.ds(a * 128, 8, stride=8), :]
                high_o[now, a] = y[pl.ds(a * 128 + 64 + 7, 8, stride=8), :]
            lows, highs = rows_ref[0], rows_ref[1]
            for q in range(4):
                a, h = q // 2, q % 2
                spot = q * 32 + now
                lows = jnp.where(lane == spot, pltpu.roll(done[(a, h, 0)], spot, 1), lows)
                highs = jnp.where(lane == spot, pltpu.roll(done[(a, h, 7)], (spot + 1) % 128, 1), highs)
            rows_ref[0] = lows
            rows_ref[1] = highs
        return carry

    lax.fori_loop(0, steps, body, 0)

    def alpha(p):
        return co[COEF[("alpha", 0, p)]]

    total = jnp.zeros((8, 128), F32)
    for p in CELLS:
        total = total + squares[AT[p]] * (alpha(p) * alpha(p))
    total = jnp.sum(jnp.sum(total, axis=1, keepdims=True), axis=0, keepdims=True)
    spread = jnp.broadcast_to(total, (8, 128))
    if first:
        square_o[...] = jnp.where(lane == 0, spread, 0.0)
    else:
        square_o[...] = jnp.where(lane == (2 if last else 1), spread, square_in[...])
    if not last:
        sub = sublanes()
        sum_o[...] = sums[...]
        final = y[...].reshape(32, 8, 128)
        final_o[...] = final if first else final + final_in[...]
        scale = {}
        for side in range(2):
            for a in range(2):
                compact = jnp.zeros((8, 128), F32)
                for j in range(8):
                    row = alpha((a, side, j))[7 * side : 7 * side + 1]
                    compact = jnp.where(sub == j, jnp.broadcast_to(row, (8, 128)), compact)
                out = high_o if side else low_o
                for n in range(steps):
                    out[n, a] = out[n, a] * compact
            spread_row = jnp.zeros((8, 128), F32)
            for q in range(4):
                a, h = q // 2, q % 2
                one = alpha((a, h, 7 * side))
                one = one[:, 127:128] if side else one[:, 0:1]
                spread_row = jnp.where(lane // 32 == q, jnp.broadcast_to(one, (8, 128)), spread_row)
            out = row_high_o if side else row_low_o
            out[...] = rows_ref[side] * spread_row
    else:
        matrix = permutation(False)
        for which, out in ((0, start_o), (1, mean_o)):
            for p in CELLS:
                a, h, j = p
                i_p = AT[p]
                if which == 0:
                    value = (final_in[i_p] + y[pl.ds(i_p * 8, 8), :]) * co[COEF[("cap", 0, p)]]
                else:
                    value = sums[i_p] * alpha(p) * (1.0 / steps)
                held[j, pl.ds(a * 16 + h, 8, stride=2), :] = value
            whole = jnp.concatenate([held[j] for j in range(8)], axis=1)
            out[...] = permute_rows(whole, matrix).reshape(2, 16, 1024)


def struct(*shape):
    return jax.ShapeDtypeStruct(shape, F32)


VM = pl.BlockSpec(memory_space=pltpu.VMEM)
SM = pl.BlockSpec(memory_space=pltpu.SMEM)
PARAMS = pltpu.CompilerParams(vmem_limit_bytes=VMEM_LIMIT)


def call(kernel, in_specs, outs, scratch):
    return pl.pallas_call(
        kernel,
        out_shape=outs,
        in_specs=in_specs,
        out_specs=[VM] * len(outs),
        scratch_shapes=scratch,
        compiler_params=PARAMS,
    )


CELL = struct(32, 8, 128)


def scratch_for(last):
    shared = [
        pltpu.VMEM((256, 128), F32),
        pltpu.VMEM((320, 128), F32),
        pltpu.VMEM((320, 128), F32),
        pltpu.VMEM((320, 128), F32),
        pltpu.VMEM((32, 8, 128), F32),
        pltpu.VMEM((32, 8, 128), F32),
    ]
    return shared + [pltpu.VMEM((8, 32, 128), F32) if last else pltpu.VMEM((2, 8, 128), F32)]


BORDERS = [struct(32, 2, 8, 128), struct(32, 2, 8, 128), struct(8, 128), struct(8, 128)]


def exchange(low, high, row_low, row_high):
    n_cols, n_rows = lax.axis_size("cols"), lax.axis_size("rows")
    cols_up = [(i, i + 1) for i in range(n_cols - 1)]
    cols_down = [(i + 1, i) for i in range(n_cols - 1)]
    rows_up = [(i, i + 1) for i in range(n_rows - 1)]
    rows_down = [(i + 1, i) for i in range(n_rows - 1)]
    from_low = lax.ppermute(high, "cols", cols_up)
    from_high = lax.ppermute(low, "cols", cols_down)
    from_row_low = lax.ppermute(row_high, "rows", rows_up)
    from_row_high = lax.ppermute(row_low, "rows", rows_down)
    return from_low, from_high, from_row_low, from_row_high


def everywhere(x, axis):
    count = lax.axis_size(axis)
    spread = jnp.broadcast_to(x[None], (count,) + x.shape)
    return jnp.sum(lax.all_to_all(spread, axis, 0, 0), axis=0)


def local(forcing, material, capacity_table, conductance_table, sink_table):
    steps = forcing.shape[0]
    n_cols, n_rows = lax.axis_size("cols"), lax.axis_size("rows")
    sizes = (16 * n_cols, 1024 * n_rows)
    place = jnp.stack([lax.axis_index("rows"), lax.axis_index("cols")]).astype(jnp.int32)
    cap, con, sink, low, high = call(
        materials_kernel,
        [SM, SM, SM, VM],
        [CELL, struct(256, 128), CELL, struct(2, 8, 128), struct(2, 8, 128)],
        [pltpu.VMEM((8, 32, 128), F32)],
    )(capacity_table, conductance_table, sink_table, material)
    grouped = con.reshape(4, 8, 8, 128)
    con_low, con_high, row_low, row_high = exchange(low, high, grouped[:, 0], grouped[:, 7])
    block = 4
    moved = pl.pallas_call(
        forcing_kernel,
        grid=(steps // block,),
        out_shape=struct(8, steps * 32, 128),
        in_specs=[pl.BlockSpec((block, 2, 16, 1024), lambda i: (i, 0, 0, 0))],
        out_specs=pl.BlockSpec((8, block * 32, 128), lambda i: (0, i, 0)),
        scratch_shapes=[pltpu.VMEM((1024, 1024), BF16)],
        compiler_params=PARAMS,
    )(forcing)
    co, sums, final, squares, *borders = call(
        functools.partial(sweep_kernel, True, False, sizes),
        [SM] + [VM] * 8,
        [struct(len(KEYS), 8, 128), CELL, CELL, struct(8, 128)] + BORDERS,
        scratch_for(False),
    )(place, cap, con, sink, con_low, con_high, row_low, row_high, moved)
    sums, final, squares, *borders = call(
        functools.partial(sweep_kernel, False, False, sizes),
        [VM] * 8,
        [CELL, CELL, struct(8, 128)] + BORDERS,
        scratch_for(False),
    )(co, sums, final, squares, *exchange(*borders))
    start, mean, squares = call(
        functools.partial(sweep_kernel, False, True, sizes),
        [VM] * 8,
        [struct(2, 16, 1024), struct(2, 16, 1024), struct(8, 128)],
        scratch_for(True),
    )(co, sums, final, squares, *exchange(*borders))
    summed = everywhere(everywhere(squares[0], "rows"), "cols")[:SWEEPS]
    count = float(steps * 2 * sizes[0] * sizes[1])
    return start, mean, jnp.sqrt(summed / count + 1e-06)


def solution(mesh):
    return jax.shard_map(
        local,
        mesh=mesh,
        in_specs=(P(None, None, "cols", "rows"), P(None, "cols", "rows"), P(), P(), P()),
        out_specs=(P(None, "cols", "rows"), P(None, "cols", "rows"), P()),
        check_vma=False,
    )
```

```python
import functools
import math

import jax
import jax.numpy as jnp
from jax import lax
from jax.experimental import pallas as pl
from jax.experimental.pallas import tpu as pltpu
from jax.sharding import PartitionSpec as P

PASSES = 8
SWEEPS = 3
F32 = jnp.float32
BF16 = jnp.bfloat16
VMEM_LIMIT = 56 * 2**20

CELLS = [(a, h, j) for a in range(2) for h in range(2) for j in range(8)]
GHOSTS = [(a, h, j) for a in range(2) for h in range(2) for j in (-1, 8)]
WIDE = CELLS + GHOSTS
CP, CM, RP, RM, VV = range(5)


def home(p):
    return (p[0], p[1], p[2] % 8)


def colour(p):
    return sum(p) % 2


UNIT = set()
for _a in range(2):
    for _h in range(2):
        for _j in range(8):
            if _j > 3:
                UNIT.add((RM, (_a, _h, _j)))
            if _j < 3:
                UNIT.add((RP, (_a, _h, _j)))
    UNIT.add((CM, (_a, 1, 3)))
UNIT.add((VV, (1, 0, 3)))

AT = {p: i for i, p in enumerate(WIDE)}
CELLS_SET = frozenset(CELLS)
KEYS = [("w", d, p) for p in WIDE for d in range(5) if (d, home(p)) not in UNIT]
KEYS += [("e", 0, p) for p in WIDE]
KEYS += [("alpha", 0, p) for p in CELLS]
KEYS += [("cap", 0, p) for p in CELLS]
KEYS += [("g", 0, p) for p in CELLS]
KEYS += [("oc", side, a) for side in range(2) for a in range(2)]
KEYS += [("or", side, q) for side in range(2) for q in range(4)]
COEF = {k: i for i, k in enumerate(KEYS)}


def lanes():
    return lax.broadcasted_iota(jnp.int32, (8, 128), 1)


def sublanes():
    return lax.broadcasted_iota(jnp.int32, (8, 128), 0)


def neighbour(x, p, d, cache):
    a, h, j = p

    def turned(source, shift):
        key = (source, shift)
        if key not in cache:
            cache[key] = pltpu.roll(x[source], shift, 0)
        return cache[key]

    if d == VV:
        return x[(1 - a, h, j)]
    if d == CP:
        return x[(a, 1, j)] if h == 0 else turned((a, 0, j), 7)
    if d == CM:
        return x[(a, 0, j)] if h == 1 else turned((a, 1, j), 1)
    return x[(a, h, j + 1)] if d == RP else x[(a, h, j - 1)]


def permutation(to_cells):
    first = lax.broadcasted_iota(jnp.int32, (256, 256), 0)
    second = lax.broadcasted_iota(jnp.int32, (256, 256), 1)
    row, spot = (first, second) if to_cells else (second, first)
    return jnp.where(row == 8 * (spot % 32) + spot // 32, 1.0, 0.0).astype(BF16)


def permute(x, matrix):
    high = x.astype(BF16)
    low = (x - high.astype(F32)).astype(BF16)
    both = jnp.dot(jnp.concatenate([high, low], axis=0), matrix, preferred_element_type=F32)
    return both[: x.shape[0]] + both[x.shape[0] :]


def materials_kernel(cap_t, con_t, sink_t, material, cap_o, con_o, sink_o, low_o, high_o, row_low_o, row_high_o, held):
    kinds = material[...].reshape(32, 1024).astype(F32).astype(BF16)
    matrix = permutation(True)
    for t in range(4):
        moved = jnp.dot(kinds[:, t * 256 : (t + 1) * 256], matrix, preferred_element_type=F32)
        for j in range(8):
            held[j, :, t * 32 : (t + 1) * 32] = moved[:, j * 32 : (j + 1) * 32]
    for p in CELLS:
        a, h, j = p
        kind = held[j, pl.ds(a * 16 + h, 8, stride=2), :]
        values = [jnp.full((8, 128), t[0], F32) for t in (cap_t, con_t, sink_t)]
        for m in range(1, 8):
            hit = kind > m - 0.5
            values = [jnp.where(hit, t[m], v) for t, v in zip((cap_t, con_t, sink_t), values)]
        i = AT[p]
        cap_o[i], con_o[pl.ds(i * 8, 8), :], sink_o[i] = values
        if j == 0:
            row_low_o[a * 2 + h] = values[1]
        if j == 7:
            row_high_o[a * 2 + h] = values[1]
    for a in range(2):
        low_o[a] = con_o[pl.ds(a * 128, 8, stride=8), :]
        high_o[a] = con_o[pl.ds(a * 128 + 64 + 7, 8, stride=8), :]


def bring(step, matrix):
    pieces = []
    for t in range(4):
        x = step[:, :, t * 256 : (t + 1) * 256].reshape(32, 256)
        high = x.astype(BF16)
        pieces += [high, (x - high.astype(F32)).astype(BF16)]
    both = jnp.dot(jnp.concatenate(pieces, axis=0), matrix, preferred_element_type=F32)
    return [both[t * 64 : t * 64 + 32] + both[t * 64 + 32 : t * 64 + 64] for t in range(4)]


def coefficients(place, sizes, cap, con, sink, con_low, con_high, row_low, row_high, co):
    n_cols, n_rows = sizes
    k = {p: con[pl.ds(AT[p] * 8, 8), :] for p in CELLS}
    row_at, col_at = place
    one, none = jnp.float32(1.0), jnp.float32(0.0)
    has_left = jnp.where(col_at > 0, one, none)
    has_right = jnp.where(col_at < n_cols // 16 - 1, one, none)
    has_before = jnp.where(row_at > 0, one, none)
    has_after = jnp.where(row_at < n_rows // 1024 - 1, one, none)
    edge_in = {}
    edge_out = {}
    lane, sub = lanes(), sublanes()

    def couple(x, y):
        return 2.0 * x * y / (x + y)

    weight = {}
    inverse = {}
    for p in CELLS:
        a, h, j = p
        q = a * 2 + h
        others = []
        if h == 0:
            others.append((k[(a, 1, j)], None))
            left = jnp.broadcast_to(con_low[a, pl.ds(j, 1), :], (8, 128)) * has_left
            others.append((jnp.where(sub == 0, left, pltpu.roll(k[(a, 1, j)], 1, 0)), sub == 0))
        else:
            right = jnp.broadcast_to(con_high[a, pl.ds(j, 1), :], (8, 128)) * has_right
            others.append((jnp.where(sub == 7, right, pltpu.roll(k[(a, 0, j)], 7, 0)), sub == 7))
            others.append((k[(a, 0, j)], None))
        if j < 7:
            others.append((k[(a, h, j + 1)], None))
        else:
            after = jnp.where(lane == 127, pltpu.roll(row_high[q], 127, 1) * has_after, pltpu.roll(k[(a, h, 0)], 127, 1))
            others.append((after, lane == 127))
        if j > 0:
            others.append((k[(a, h, j - 1)], None))
        else:
            before = jnp.where(lane == 0, pltpu.roll(row_low[q], 1, 1) * has_before, pltpu.roll(k[(a, h, 7)], 1, 1))
            others.append((before, lane == 0))
        others.append((k[(1 - a, h, j)], None))
        edges = [couple(k[p], other) for other, _ in others]
        capacity = cap[AT[p]]
        diagonal = capacity + sink[AT[p]]
        for e in edges:
            diagonal = diagonal + e
        inverse[p] = 1.0 / diagonal
        for d, (e, (_, mask)) in enumerate(zip(edges, others)):
            e = e * inverse[p]
            edge_in[d, p] = e if mask is None else jnp.where(mask, 0.0, e)
            edge_out[d, p] = None if mask is None else jnp.where(mask, e, 0.0)
    alpha = {(0, 0, 3): jnp.ones((8, 128), F32)}
    alpha[(1, 0, 3)] = edge_in[VV, (1, 0, 3)] * alpha[(0, 0, 3)]
    for a in range(2):
        alpha[(a, 1, 3)] = edge_in[CM, (a, 1, 3)] * alpha[(a, 0, 3)]
        for h in range(2):
            for j in range(4, 8):
                alpha[(a, h, j)] = edge_in[RM, (a, h, j)] * alpha[(a, h, j - 1)]
            for j in (2, 1, 0):
                alpha[(a, h, j)] = edge_in[RP, (a, h, j)] * alpha[(a, h, j + 1)]
    for a in range(2):
        for h in range(2):
            alpha[(a, h, -1)] = pltpu.roll(alpha[(a, h, 7)], 1, 1)
            alpha[(a, h, 8)] = pltpu.roll(alpha[(a, h, 0)], 127, 1)

    def put(kind, d, p, value):
        co[COEF[(kind, d, p)]] = value

    cache = {}
    column0 = (col_at * 16).astype(F32)
    row0 = (row_at * 1024).astype(F32)
    scaled_out = {}
    for p in CELLS:
        a, h, j = p
        over = 1.0 / alpha[p]
        put("alpha", 0, p, alpha[p])
        put("cap", 0, p, cap[AT[p]] * alpha[p])
        e = cap[AT[p]] * inverse[p] - 1.0
        put("e", 0, p, e)
        column = (2 * sub + h).astype(F32) + column0
        row = (8 * lane + j).astype(F32) + row0
        profile = jnp.exp(math.log(3.0) * (column * (1.0 / n_cols) + row * (1.0 / n_rows)))
        put("g", 0, p, profile * inverse[p] * over)
        if j == 7:
            put("e", 0, (a, h, -1), pltpu.roll(e, 1, 1))
        if j == 0:
            put("e", 0, (a, h, 8), pltpu.roll(e, 127, 1))
        for d in range(5):
            if edge_out[d, p] is not None:
                scaled_out[d, p] = edge_out[d, p] * over
            if (d, p) in UNIT:
                continue
            w = edge_in[d, p] * neighbour(alpha, p, d, cache) * over
            put("w", d, p, w)
            if j == 7:
                put("w", d, (a, h, -1), pltpu.roll(w, 1, 1))
            if j == 0:
                put("w", d, (a, h, 8), pltpu.roll(w, 127, 1))
    for a in range(2):
        low, high = jnp.zeros((8, 128), F32), jnp.zeros((8, 128), F32)
        for j in range(8):
            low = jnp.where(sub == j, jnp.broadcast_to(scaled_out[CM, (a, 0, j)][0:1], (8, 128)), low)
            high = jnp.where(sub == j, jnp.broadcast_to(scaled_out[CP, (a, 1, j)][7:8], (8, 128)), high)
        put("oc", 0, a, low)
        put("oc", 1, a, high)
        for h in range(2):
            put("or", 0, a * 2 + h, scaled_out[RM, (a, h, 0)])
            put("or", 1, a * 2 + h, scaled_out[RP, (a, h, 7)])


SKEW = True


def rows_of(p):
    return pl.ds(AT[p] * 8, 8)


def time_step(source, extra, co, held):
    def applied(x, p, cache, memo):
        total = None
        for d in (VV, CP, CM, RP, RM):
            term = neighbour(x, p, d, cache)
            if (d, home(p)) not in UNIT:
                if d not in memo:
                    memo[d] = co[COEF[("w", d, p)]]
                term = memo[d] * term
            total = term if total is None else total + term
        return total

    def add_ghosts(x):
        for a, h, j in list(x):
            if j >= 6:
                x[(a, h, j - 8)] = pltpu.roll(x[(a, h, j)], 1, 1)
            if j <= 1:
                x[(a, h, j + 8)] = pltpu.roll(x[(a, h, j)], 127, 1)

    start = [{p: held[0][rows_of(p), :] for p in CELLS if colour(p) == c} for c in range(2)]
    for c in range(2):
        add_ghosts(start[c])
    fields = [dict(start[0]), dict(start[1])]
    lag = 1 if SKEW else 0
    for stage in range(1, PASSES + 1 + lag):
        jobs = []
        for chain in (1, 0):
            k = stage - chain * lag
            if 1 <= k <= PASSES:
                wide = k % 2 == 1
                if wide and k > 1:
                    add_ghosts(fields[chain])
                jobs.append((chain, k, wide, (chain + k) % 2, {}, {}))
        memos = {}
        for p in WIDE:
            for chain, k, wide, to, cache, out in jobs:
                if colour(p) != to or (not wide and p not in CELLS_SET):
                    continue
                value = applied(fields[chain], p, cache, memos.setdefault(p, {}))
                if k == 1:
                    base = source(p) + co[COEF[("e", 0, p)]] * start[to][p]
                    if extra is not None and p in extra:
                        base = base + extra[p]
                    value = value + base
                elif k == 2:
                    value = value + held[1][rows_of(p), :]
                elif k == 4:
                    value = value + held[2][rows_of(p), :]
                elif k == 8:
                    value = value + (held[3][rows_of(p), :] + held[0][rows_of(p), :])
                if k == 1 and p in CELLS_SET:
                    held[1][rows_of(p), :] = value
                elif k in (2, 4):
                    held[k // 2 + 1][rows_of(p), :] = value
                out[p] = value
        for chain, k, wide, to, cache, out in jobs:
            fields[chain] = out
    return {**fields[0], **fields[1]}


def sweep_kernel(first, last, sizes, *refs):
    refs = list(refs)
    if first:
        (cap, con, sink, con_low, con_high, row_low, row_high, forcing) = refs[:8]
        co = refs[8]
        refs = refs[9:]
        place = (lax.axis_index("rows"), lax.axis_index("cols"))
        (matrix, raw, force, arrived) = refs[-4:]
        refs = refs[:-4]
        copy = pltpu.make_async_copy(forcing, raw, arrived)
        copy.start()
        matrix[...] = permutation(True)
        coefficients(place, sizes, cap, con, sink, con_low, con_high, row_low, row_high, co)
        copy.wait()

        def fetch(now, slot):
            for t, block in enumerate(bring(raw[now], matrix[...])):
                for j in range(8):
                    force[slot, j, :, t * 32 : (t + 1) * 32] = block[:, j * 32 : (j + 1) * 32]

        fetch(31, 1)
    else:
        (co, sum_in, final_in, square_in, got_low, got_high, got_row_low, got_row_high) = refs[:8]
        refs = refs[8:]
    if last:
        (start_o, mean_o, square_o, fields, f_ref, sums, squares, held) = refs
    else:
        (sum_o, final_o, square_o, low_o, high_o, row_low_o, row_high_o) = refs[:7]
        (fields, f_ref, sums, squares, rows_ref) = refs[7:]
    steps = 32
    fields[...] = jnp.zeros_like(fields)
    stages = [fields.at[k] for k in range(4)]
    y = stages[0]
    squares[...] = jnp.zeros_like(squares)
    if first:
        sums[...] = jnp.zeros_like(sums)
    else:
        sums[...] = sum_in[...]
        f_ref[...] = jnp.zeros_like(f_ref)
    if not last:
        rows_ref[...] = jnp.zeros_like(rows_ref)
    lane = lanes()

    def one(now, slot):
        extra = None
        if first:
            memo = {}

            def source(p):
                a, h, j = home(p)
                if (a, h, j) not in memo:
                    rows = pl.ds(a * 16 + h, 8, stride=2)
                    memo[(a, h, j)] = force[slot, j, rows, :] * co[COEF[("g", 0, (a, h, j))]]
                value = memo[(a, h, j)]
                if p[2] == -1:
                    value = pltpu.roll(value, 1, 1)
                if p[2] == 8:
                    value = pltpu.roll(value, 127, 1)
                return value

        else:
            extra = {}
            for side, got in enumerate((got_low, got_high)):
                for a in range(2):
                    value = got[now, a] * co[COEF[("oc", side, a)]]
                    base = (a * 2 + side) * 64
                    s = 7 * side
                    f_ref[pl.ds(base + s, 8, stride=8), :] = value
                    f_ref[pl.ds(AT[(a, side, -1)] * 8 + s, 1), :] = pltpu.roll(value, 1, 1)[7:8]
                    f_ref[pl.ds(AT[(a, side, 8)] * 8 + s, 1), :] = pltpu.roll(value, 127, 1)[0:1]
            for q in range(4):
                a, h = q // 2, q % 2
                spot = q * 32 + now
                extra[(a, h, 0)] = co[COEF[("or", 0, q)]] * pltpu.roll(got_row_low[...], (128 - spot) % 128, 1)
                extra[(a, h, 7)] = co[COEF[("or", 1, q)]] * pltpu.roll(got_row_high[...], 127 - spot, 1)

            def source(p):
                return f_ref[pl.ds(AT[p] * 8, 8), :]

        done = time_step(source, extra, co, stages)
        if first:
            fetch(jnp.maximum(now - 1, 0), 1 - slot)
        for p in CELLS:
            i_p = AT[p]
            x = done[p]
            y[rows_of(p), :] = x
            sums[i_p] += x
            squares[i_p] += x * x
        if not last:
            for a in range(2):
                low_o[now, a] = y[pl.ds(a * 128, 8, stride=8), :]
                high_o[now, a] = y[pl.ds(a * 128 + 64 + 7, 8, stride=8), :]
            lows, highs = rows_ref[0], rows_ref[1]
            for q in range(4):
                a, h = q // 2, q % 2
                spot = q * 32 + now
                lows = jnp.where(lane == spot, pltpu.roll(done[(a, h, 0)], spot, 1), lows)
                highs = jnp.where(lane == spot, pltpu.roll(done[(a, h, 7)], (spot + 1) % 128, 1), highs)
            rows_ref[0] = lows
            rows_ref[1] = highs

    def body(i, carry):
        one(steps - 1 - 2 * i, 1)
        one(steps - 2 - 2 * i, 0)
        return carry

    lax.fori_loop(0, steps // 2, body, 0)

    def alpha(p):
        return co[COEF[("alpha", 0, p)]]

    total = jnp.zeros((8, 128), F32)
    for p in CELLS:
        total = total + squares[AT[p]] * (alpha(p) * alpha(p))
    total = jnp.sum(jnp.sum(total, axis=1, keepdims=True), axis=0, keepdims=True)
    spread = jnp.broadcast_to(total, (8, 128))
    if first:
        square_o[...] = jnp.where(lane == 0, spread, 0.0)
    else:
        square_o[...] = jnp.where(lane == (2 if last else 1), spread, square_in[...])
    if not last:
        sub = sublanes()
        sum_o[...] = sums[...]
        final = y[...].reshape(32, 8, 128)
        final_o[...] = final if first else final + final_in[...]
        scale = {}
        for side in range(2):
            for a in range(2):
                compact = jnp.zeros((8, 128), F32)
                for j in range(8):
                    row = alpha((a, side, j))[7 * side : 7 * side + 1]
                    compact = jnp.where(sub == j, jnp.broadcast_to(row, (8, 128)), compact)
                out = high_o if side else low_o
                for n in range(steps):
                    out[n, a] = out[n, a] * compact
            spread_row = jnp.zeros((8, 128), F32)
            for q in range(4):
                a, h = q // 2, q % 2
                one = alpha((a, h, 7 * side))
                one = one[:, 127:128] if side else one[:, 0:1]
                spread_row = jnp.where(lane // 32 == q, jnp.broadcast_to(one, (8, 128)), spread_row)
            out = row_high_o if side else row_low_o
            out[...] = rows_ref[side] * spread_row
    else:
        matrix = permutation(False)
        for which, out in ((0, start_o), (1, mean_o)):
            for p in CELLS:
                a, h, j = p
                i_p = AT[p]
                if which == 0:
                    value = (final_in[i_p] + y[rows_of(p), :]) * co[COEF[("cap", 0, p)]]
                else:
                    value = sums[i_p] * alpha(p) * (1.0 / steps)
                held[j, pl.ds(a * 16 + h, 8, stride=2), :] = value
            for t in range(4):
                piece = jnp.concatenate([held[j, :, t * 32 : (t + 1) * 32] for j in range(8)], axis=1)
                out[:, :, t * 256 : (t + 1) * 256] = permute(piece, matrix).reshape(2, 16, 256)


def struct(*shape):
    return jax.ShapeDtypeStruct(shape, F32)


VM = pl.BlockSpec(memory_space=pltpu.VMEM)
SM = pl.BlockSpec(memory_space=pltpu.SMEM)
PARAMS = pltpu.CompilerParams(vmem_limit_bytes=VMEM_LIMIT)


def call(kernel, in_specs, outs, scratch):
    return pl.pallas_call(
        kernel,
        out_shape=outs,
        in_specs=in_specs,
        out_specs=[VM] * len(outs),
        scratch_shapes=scratch,
        compiler_params=PARAMS,
    )


CELL = struct(32, 8, 128)


def scratch_for(last):
    shared = [
        pltpu.VMEM((4, 256, 128), F32),
        pltpu.VMEM((320, 128), F32),
        pltpu.VMEM((32, 8, 128), F32),
        pltpu.VMEM((32, 8, 128), F32),
    ]
    return shared + [pltpu.VMEM((8, 32, 128), F32) if last else pltpu.VMEM((2, 8, 128), F32)]


FORCING = [
    pltpu.VMEM((256, 256), BF16),
    pltpu.VMEM((32, 2, 16, 1024), F32),
    pltpu.VMEM((2, 8, 32, 128), F32),
    pltpu.SemaphoreType.DMA,
]
BORDERS = [struct(32, 2, 8, 128), struct(32, 2, 8, 128), struct(8, 128), struct(8, 128)]


def exchange(low, high, row_low, row_high):
    n_cols, n_rows = lax.axis_size("cols"), lax.axis_size("rows")
    cols_up = [(i, (i + 1) % n_cols) for i in range(n_cols)]
    cols_down = [(j, i) for i, j in cols_up]
    rows_up = [(i, (i + 1) % n_rows) for i in range(n_rows)]
    rows_down = [(j, i) for i, j in rows_up]
    from_low = lax.ppermute(high, "cols", cols_up)
    from_high = lax.ppermute(low, "cols", cols_down)
    from_row_low = lax.ppermute(row_high, "rows", rows_up)
    from_row_high = lax.ppermute(row_low, "rows", rows_down)
    return from_low, from_high, from_row_low, from_row_high


def everywhere(x, axis):
    count = lax.axis_size(axis)
    spread = jnp.broadcast_to(x[None], (count,) + x.shape)
    return jnp.sum(lax.all_to_all(spread, axis, 0, 0), axis=0)


def local(forcing, material, capacity_table, conductance_table, sink_table):
    steps = forcing.shape[0]
    n_cols, n_rows = lax.axis_size("cols"), lax.axis_size("rows")
    sizes = (16 * n_cols, 1024 * n_rows)
    cap, con, sink, *facing = call(
        materials_kernel,
        [SM, SM, SM, VM],
        [CELL, struct(256, 128), CELL] + [struct(2, 8, 128)] * 2 + [struct(4, 8, 128)] * 2,
        [pltpu.VMEM((8, 32, 128), F32)],
    )(capacity_table, conductance_table, sink_table, material)
    con_low, con_high, row_low, row_high = exchange(*facing)
    co, sums, final, squares, *borders = call(
        functools.partial(sweep_kernel, True, False, sizes),
        [VM] * 7 + [pl.BlockSpec(memory_space=pl.ANY)],
        [struct(len(KEYS), 8, 128), CELL, CELL, struct(8, 128)] + BORDERS,
        scratch_for(False) + FORCING,
    )(cap, con, sink, con_low, con_high, row_low, row_high, forcing)
    sums, final, squares, *borders = call(
        functools.partial(sweep_kernel, False, False, sizes),
        [VM] * 8,
        [CELL, CELL, struct(8, 128)] + BORDERS,
        scratch_for(False),
    )(co, sums, final, squares, *exchange(*borders))
    start, mean, squares = call(
        functools.partial(sweep_kernel, False, True, sizes),
        [VM] * 8,
        [struct(2, 16, 1024), struct(2, 16, 1024), struct(8, 128)],
        scratch_for(True),
    )(co, sums, final, squares, *exchange(*borders))
    summed = everywhere(everywhere(squares[0], "rows"), "cols")[:SWEEPS]
    count = float(steps * 2 * sizes[0] * sizes[1])
    return start, mean, jnp.sqrt(summed / count + 1e-06)


def solution(mesh):
    return jax.shard_map(
        local,
        mesh=mesh,
        in_specs=(P(None, None, "cols", "rows"), P(None, "cols", "rows"), P(), P(), P()),
        out_specs=(P(None, "cols", "rows"), P(None, "cols", "rows"), P()),
        check_vma=False,
    )
```

```python
import functools

import jax
import jax.numpy as jnp
from jax import lax
from jax.experimental import pallas as pl
from jax.experimental.pallas import tpu as pltpu
from jax.sharding import PartitionSpec as P

PASSES = 8
SWEEPS = 3
F32 = jnp.float32
BF16 = jnp.bfloat16
VMEM_LIMIT = 24 * 2**20

CELLS = [(a, h, j) for a in range(2) for h in range(2) for j in range(8)]
GHOSTS = [(a, h, j) for a in range(2) for h in range(2) for j in (-1, 8)]
WIDE = CELLS + GHOSTS
CP, CM, RP, RM, VV = range(5)


def home(p):
    return (p[0], p[1], p[2] % 8)


def colour(p):
    return sum(p) % 2


UNIT = set()
for _a in range(2):
    for _h in range(2):
        for _j in range(8):
            if _j > 3:
                UNIT.add((RM, (_a, _h, _j)))
            if _j < 3:
                UNIT.add((RP, (_a, _h, _j)))
    UNIT.add((CM, (_a, 1, 3)))
UNIT.add((VV, (1, 0, 3)))

AT = {p: i for i, p in enumerate(WIDE)}
CELLS_SET = frozenset(CELLS)
KEYS = [("w", d, p) for p in WIDE for d in range(5) if (d, home(p)) not in UNIT]
KEYS += [("e", 0, p) for p in WIDE]
KEYS += [("alpha", 0, p) for p in CELLS]
KEYS += [("cap", 0, p) for p in CELLS]
KEYS += [("g", 0, p) for p in CELLS]
KEYS += [("oc", side, a) for side in range(2) for a in range(2)]
KEYS += [("or", side, q) for side in range(2) for q in range(4)]
COEF = {k: i for i, k in enumerate(KEYS)}


def lanes():
    return lax.broadcasted_iota(jnp.int32, (8, 128), 1)


def sublanes():
    return lax.broadcasted_iota(jnp.int32, (8, 128), 0)


def neighbour(x, p, d, cache):
    a, h, j = p

    def turned(source, shift):
        key = (source, shift)
        if key not in cache:
            cache[key] = pltpu.roll(x[source], shift, 0)
        return cache[key]

    if d == VV:
        return x[(1 - a, h, j)]
    if d == CP:
        return x[(a, 1, j)] if h == 0 else turned((a, 0, j), 7)
    if d == CM:
        return x[(a, 0, j)] if h == 1 else turned((a, 1, j), 1)
    return x[(a, h, j + 1)] if d == RP else x[(a, h, j - 1)]


def permutation(to_cells):
    first = lax.broadcasted_iota(jnp.int32, (256, 256), 0)
    second = lax.broadcasted_iota(jnp.int32, (256, 256), 1)
    row, spot = (first, second) if to_cells else (second, first)
    return jnp.where(row == 8 * (spot % 32) + spot // 32, 1.0, 0.0).astype(BF16)


def permute(x, matrix):
    high = x.astype(BF16)
    low = (x - high.astype(F32)).astype(BF16)
    both = jnp.dot(jnp.concatenate([high, low], axis=0), matrix, preferred_element_type=F32)
    return both[: x.shape[0]] + both[x.shape[0] :]


def materials_kernel(*refs):
    (tables_in, material_in, cap_o, con_o, sink_o, low_o, high_o, row_low_o, row_high_o, held, tables, material) = refs[:12]
    arrived = refs[12]
    copies = [
        pltpu.make_async_copy(tables_in, tables, arrived.at[0]),
        pltpu.make_async_copy(material_in, material, arrived.at[1]),
    ]
    for copy in copies:
        copy.start()
    for copy in copies:
        copy.wait()
    kinds = material[...].reshape(32, 1024).astype(F32).astype(BF16)
    matrix = permutation(True)
    for t in range(4):
        moved = jnp.dot(kinds[:, t * 256 : (t + 1) * 256], matrix, preferred_element_type=F32)
        for j in range(8):
            held[j, :, t * 32 : (t + 1) * 32] = moved[:, j * 32 : (j + 1) * 32]
    for p in CELLS:
        a, h, j = p
        kind = held[j, pl.ds(a * 16 + h, 8, stride=2), :]
        values = [jnp.full((8, 128), tables[t, 0], F32) for t in range(3)]
        for m in range(1, 8):
            hit = kind > m - 0.5
            values = [jnp.where(hit, tables[t, m], v) for t, v in enumerate(values)]
        i = AT[p]
        cap_o[i], con_o[pl.ds(i * 8, 8), :], sink_o[i] = values
        if j == 0:
            row_low_o[a * 2 + h] = values[1]
        if j == 7:
            row_high_o[a * 2 + h] = values[1]
    for a in range(2):
        low_o[a] = con_o[pl.ds(a * 128, 8, stride=8), :]
        high_o[a] = con_o[pl.ds(a * 128 + 64 + 7, 8, stride=8), :]


def bring(step, matrix):
    pieces = []
    for t in range(4):
        x = step[:, :, t * 256 : (t + 1) * 256].reshape(32, 256)
        high = x.astype(BF16)
        pieces += [high, (x - high.astype(F32)).astype(BF16)]
    both = jnp.dot(jnp.concatenate(pieces, axis=0), matrix, preferred_element_type=F32)
    return [both[t * 64 : t * 64 + 32] + both[t * 64 + 32 : t * 64 + 64] for t in range(4)]


def coefficients(place, sizes, cap, con, sink, con_low, con_high, row_low, row_high, co):
    n_cols, n_rows = sizes
    k = {p: con[pl.ds(AT[p] * 8, 8), :] for p in CELLS}
    row_at, col_at = place
    one, none = jnp.float32(1.0), jnp.float32(0.0)
    has_left = jnp.where(col_at > 0, one, none)
    has_right = jnp.where(col_at < n_cols // 16 - 1, one, none)
    has_before = jnp.where(row_at > 0, one, none)
    has_after = jnp.where(row_at < n_rows // 1024 - 1, one, none)
    edge_in = {}
    edge_out = {}
    lane, sub = lanes(), sublanes()

    def couple(x, y):
        return 2.0 * x * y / (x + y)

    weight = {}
    inverse = {}
    for p in CELLS:
        a, h, j = p
        q = a * 2 + h
        others = []
        if h == 0:
            others.append((k[(a, 1, j)], None))
            left = jnp.broadcast_to(con_low[a, pl.ds(j, 1), :], (8, 128)) * has_left
            others.append((jnp.where(sub == 0, left, pltpu.roll(k[(a, 1, j)], 1, 0)), sub == 0))
        else:
            right = jnp.broadcast_to(con_high[a, pl.ds(j, 1), :], (8, 128)) * has_right
            others.append((jnp.where(sub == 7, right, pltpu.roll(k[(a, 0, j)], 7, 0)), sub == 7))
            others.append((k[(a, 0, j)], None))
        if j < 7:
            others.append((k[(a, h, j + 1)], None))
        else:
            after = jnp.where(lane == 127, pltpu.roll(row_high[q], 127, 1) * has_after, pltpu.roll(k[(a, h, 0)], 127, 1))
            others.append((after, lane == 127))
        if j > 0:
            others.append((k[(a, h, j - 1)], None))
        else:
            before = jnp.where(lane == 0, pltpu.roll(row_low[q], 1, 1) * has_before, pltpu.roll(k[(a, h, 7)], 1, 1))
            others.append((before, lane == 0))
        others.append((k[(1 - a, h, j)], None))
        edges = [couple(k[p], other) for other, _ in others]
        capacity = cap[AT[p]]
        diagonal = capacity + sink[AT[p]]
        for e in edges:
            diagonal = diagonal + e
        inverse[p] = 1.0 / diagonal
        for d, (e, (_, mask)) in enumerate(zip(edges, others)):
            e = e * inverse[p]
            edge_in[d, p] = e if mask is None else jnp.where(mask, 0.0, e)
            edge_out[d, p] = None if mask is None else jnp.where(mask, e, 0.0)
    alpha = {(0, 0, 3): jnp.ones((8, 128), F32)}
    alpha[(1, 0, 3)] = edge_in[VV, (1, 0, 3)] * alpha[(0, 0, 3)]
    for a in range(2):
        alpha[(a, 1, 3)] = edge_in[CM, (a, 1, 3)] * alpha[(a, 0, 3)]
        for h in range(2):
            for j in range(4, 8):
                alpha[(a, h, j)] = edge_in[RM, (a, h, j)] * alpha[(a, h, j - 1)]
            for j in (2, 1, 0):
                alpha[(a, h, j)] = edge_in[RP, (a, h, j)] * alpha[(a, h, j + 1)]
    for a in range(2):
        for h in range(2):
            alpha[(a, h, -1)] = pltpu.roll(alpha[(a, h, 7)], 1, 1)
            alpha[(a, h, 8)] = pltpu.roll(alpha[(a, h, 0)], 127, 1)

    def put(kind, d, p, value):
        co[COEF[(kind, d, p)]] = value

    cache = {}
    scaled_out = {}
    for p in CELLS:
        a, h, j = p
        over = 1.0 / alpha[p]
        put("alpha", 0, p, alpha[p])
        put("cap", 0, p, cap[AT[p]] * alpha[p])
        e = cap[AT[p]] * inverse[p] - 1.0
        put("e", 0, p, e)
        put("g", 0, p, inverse[p] * over)
        if j == 7:
            put("e", 0, (a, h, -1), pltpu.roll(e, 1, 1))
        if j == 0:
            put("e", 0, (a, h, 8), pltpu.roll(e, 127, 1))
        for d in range(5):
            if edge_out[d, p] is not None:
                scaled_out[d, p] = edge_out[d, p] * over
            if (d, p) in UNIT:
                continue
            w = edge_in[d, p] * neighbour(alpha, p, d, cache) * over
            put("w", d, p, w)
            if j == 7:
                put("w", d, (a, h, -1), pltpu.roll(w, 1, 1))
            if j == 0:
                put("w", d, (a, h, 8), pltpu.roll(w, 127, 1))
    for a in range(2):
        low, high = jnp.zeros((8, 128), F32), jnp.zeros((8, 128), F32)
        for j in range(8):
            low = jnp.where(sub == j, jnp.broadcast_to(scaled_out[CM, (a, 0, j)][0:1], (8, 128)), low)
            high = jnp.where(sub == j, jnp.broadcast_to(scaled_out[CP, (a, 1, j)][7:8], (8, 128)), high)
        put("oc", 0, a, low)
        put("oc", 1, a, high)
        for h in range(2):
            put("or", 0, a * 2 + h, scaled_out[RM, (a, h, 0)])
            put("or", 1, a * 2 + h, scaled_out[RP, (a, h, 7)])


SKEW = True


def rows_of(p):
    return pl.ds(AT[p] * 8, 8)


def time_step(source, extra, co, held):
    def applied(x, p, cache, memo):
        total = None
        for d in (VV, CP, CM, RP, RM):
            term = neighbour(x, p, d, cache)
            if (d, home(p)) not in UNIT:
                if d not in memo:
                    memo[d] = co[COEF[("w", d, p)]]
                term = memo[d] * term
            total = term if total is None else total + term
        return total

    def add_ghosts(x):
        for a, h, j in list(x):
            if j >= 6:
                x[(a, h, j - 8)] = pltpu.roll(x[(a, h, j)], 1, 1)
            if j <= 1:
                x[(a, h, j + 8)] = pltpu.roll(x[(a, h, j)], 127, 1)

    start = [{p: held[0][rows_of(p), :] for p in CELLS if colour(p) == c} for c in range(2)]
    for c in range(2):
        add_ghosts(start[c])
    fields = [dict(start[0]), dict(start[1])]
    lag = 1 if SKEW else 0
    for stage in range(1, PASSES + 1 + lag):
        jobs = []
        for chain in (1, 0):
            k = stage - chain * lag
            if 1 <= k <= PASSES:
                wide = k % 2 == 1
                if wide and k > 1:
                    add_ghosts(fields[chain])
                jobs.append((chain, k, wide, (chain + k) % 2, {}, {}))
        memos = {}
        for p in WIDE:
            for chain, k, wide, to, cache, out in jobs:
                if colour(p) != to or (not wide and p not in CELLS_SET):
                    continue
                value = applied(fields[chain], p, cache, memos.setdefault(p, {}))
                if k == 1:
                    base = source(p) + co[COEF[("e", 0, p)]] * start[to][p]
                    if extra is not None and p in extra:
                        base = base + extra[p]
                    value = value + base
                elif k == 2:
                    value = value + held[1][rows_of(p), :]
                elif k == 4:
                    value = value + held[2][rows_of(p), :]
                elif k == 8:
                    value = value + (held[3][rows_of(p), :] + held[0][rows_of(p), :])
                if k == 1 and p in CELLS_SET:
                    held[1][rows_of(p), :] = value
                elif k in (2, 4):
                    held[k // 2 + 1][rows_of(p), :] = value
                out[p] = value
        for chain, k, wide, to, cache, out in jobs:
            fields[chain] = out
    return {**fields[0], **fields[1]}


def sweep_kernel(first, last, sizes, *refs):
    refs = list(refs)
    if first:
        (cap, con, sink, con_low, con_high, row_low, row_high, forcing) = refs[:8]
        co = refs[8]
        refs = refs[9:]
        place = (lax.axis_index("rows"), lax.axis_index("cols"))
        (matrix, force) = refs[-2:]
        refs = refs[:-2]
        matrix[...] = permutation(True)
        coefficients(place, sizes, cap, con, sink, con_low, con_high, row_low, row_high, co)

        def fetch(now, slot):
            for t, block in enumerate(bring(forcing[now], matrix[...])):
                for j in range(8):
                    force[slot, j, :, t * 32 : (t + 1) * 32] = block[:, j * 32 : (j + 1) * 32]

        fetch(31, 1)
    else:
        (co, sum_in, final_in, square_in, got_near, got_far, got_row_low, got_row_high) = refs[:8]
        refs = refs[8:]
    if last:
        (start_o, mean_o, square_o, fields, f_ref, sums, squares, held) = refs
    else:
        (sum_o, final_o, square_o, near_o, far_o, row_low_o, row_high_o) = refs[:7]
        (fields, f_ref, sums, squares, rows_ref) = refs[7:]
    steps = 32
    fields[...] = jnp.zeros_like(fields)
    stages = [fields.at[k] for k in range(4)]
    y = stages[0]
    squares[...] = jnp.zeros_like(squares)
    if first:
        sums[...] = jnp.zeros_like(sums)
    else:
        sums[...] = sum_in[...]
        f_ref[...] = jnp.zeros_like(f_ref)
    if not last:
        rows_ref[...] = jnp.zeros_like(rows_ref)
    lane = lanes()

    even = lax.axis_index("cols") % 2 == 0

    def record(at):
        for a in range(2):
            low = y[pl.ds(a * 128, 8, stride=8), :]
            high = y[pl.ds(a * 128 + 64 + 7, 8, stride=8), :]
            near_o[at, a] = jnp.where(even, high, low)
            far_o[at, a] = jnp.where(even, low, high)
        lows, highs = rows_ref[0], rows_ref[1]
        for q in range(4):
            a, h = q // 2, q % 2
            spot = q * 32 + at
            lows = jnp.where(lane == spot, pltpu.roll(y[rows_of((a, h, 0)), :], spot, 1), lows)
            highs = jnp.where(lane == spot, pltpu.roll(y[rows_of((a, h, 7)), :], (spot + 1) % 128, 1), highs)
        rows_ref[0] = lows
        rows_ref[1] = highs

    def one(now, slot):
        if not last:
            record(jnp.minimum(now + 1, steps - 1))
        extra = None
        if first:
            memo = {}

            def source(p):
                a, h, j = home(p)
                if (a, h, j) not in memo:
                    rows = pl.ds(a * 16 + h, 8, stride=2)
                    memo[(a, h, j)] = force[slot, j, rows, :] * co[COEF[("g", 0, (a, h, j))]]
                value = memo[(a, h, j)]
                if p[2] == -1:
                    value = pltpu.roll(value, 1, 1)
                if p[2] == 8:
                    value = pltpu.roll(value, 127, 1)
                return value

        else:
            extra = {}
            for side in range(2):
                for a in range(2):
                    near, far = got_near[now, a], got_far[now, a]
                    got = jnp.where(even, near, far) if side else jnp.where(even, far, near)
                    value = got * co[COEF[("oc", side, a)]]
                    base = (a * 2 + side) * 64
                    s = 7 * side
                    f_ref[pl.ds(base + s, 8, stride=8), :] = value
                    f_ref[pl.ds(AT[(a, side, -1)] * 8 + s, 1), :] = pltpu.roll(value, 1, 1)[7:8]
                    f_ref[pl.ds(AT[(a, side, 8)] * 8 + s, 1), :] = pltpu.roll(value, 127, 1)[0:1]
            for q in range(4):
                a, h = q // 2, q % 2
                spot = q * 32 + now
                extra[(a, h, 0)] = co[COEF[("or", 0, q)]] * pltpu.roll(got_row_low[...], (128 - spot) % 128, 1)
                extra[(a, h, 7)] = co[COEF[("or", 1, q)]] * pltpu.roll(got_row_high[...], 127 - spot, 1)

            def source(p):
                return f_ref[pl.ds(AT[p] * 8, 8), :]

        done = time_step(source, extra, co, stages)
        if first:
            fetch(jnp.maximum(now - 1, 0), 1 - slot)
        for p in CELLS:
            i_p = AT[p]
            x = done[p]
            y[rows_of(p), :] = x
            sums[i_p] += x
            squares[i_p] += x * x
    def body(i, carry):
        one(steps - 1 - 2 * i, 1)
        one(steps - 2 - 2 * i, 0)
        return carry

    lax.fori_loop(0, steps // 2, body, 0)
    if not last:
        record(0)

    def alpha(p):
        return co[COEF[("alpha", 0, p)]]

    total = jnp.zeros((8, 128), F32)
    for p in CELLS:
        total = total + squares[AT[p]] * (alpha(p) * alpha(p))
    total = jnp.sum(jnp.sum(total, axis=1, keepdims=True), axis=0, keepdims=True)
    spread = jnp.broadcast_to(total, (8, 128))
    if first:
        square_o[...] = jnp.where(lane == 0, spread, 0.0)
    else:
        spread = jnp.where(lane == (2 if last else 1), spread, square_in[...])
        if last:
            for n in range(square_o.shape[0]):
                square_o[n] = spread[0:1]
        else:
            square_o[...] = spread
    if not last:
        sub = sublanes()
        sum_o[...] = sums[...]
        final = y[...].reshape(32, 8, 128)
        final_o[...] = final if first else final + final_in[...]
        for a in range(2):
            scale = []
            for side in range(2):
                compact = jnp.zeros((8, 128), F32)
                for j in range(8):
                    row = alpha((a, side, j))[7 * side : 7 * side + 1]
                    compact = jnp.where(sub == j, jnp.broadcast_to(row, (8, 128)), compact)
                scale.append(compact)
            near_scale = jnp.where(even, scale[1], scale[0])
            far_scale = jnp.where(even, scale[0], scale[1])
            for n in range(steps):
                near_o[n, a] = near_o[n, a] * near_scale
                far_o[n, a] = far_o[n, a] * far_scale
        for side in range(2):
            spread_row = jnp.zeros((8, 128), F32)
            for q in range(4):
                a, h = q // 2, q % 2
                one = alpha((a, h, 7 * side))
                one = one[:, 127:128] if side else one[:, 0:1]
                spread_row = jnp.where(lane // 32 == q, jnp.broadcast_to(one, (8, 128)), spread_row)
            out = row_high_o if side else row_low_o
            out[...] = rows_ref[side] * spread_row
    else:
        matrix = permutation(False)
        for which, out in ((0, start_o), (1, mean_o)):
            for p in CELLS:
                a, h, j = p
                i_p = AT[p]
                if which == 0:
                    value = (final_in[i_p] + y[rows_of(p), :]) * co[COEF[("cap", 0, p)]]
                else:
                    value = sums[i_p] * alpha(p) * (1.0 / steps)
                held[j, pl.ds(a * 16 + h, 8, stride=2), :] = value
            for t in range(4):
                piece = jnp.concatenate([held[j, :, t * 32 : (t + 1) * 32] for j in range(8)], axis=1)
                out[:, :, t * 256 : (t + 1) * 256] = permute(piece, matrix).reshape(2, 16, 256)


def struct(*shape):
    return jax.ShapeDtypeStruct(shape, F32)


VM = pl.BlockSpec(memory_space=pltpu.VMEM)
HBM = pl.BlockSpec(memory_space=pltpu.HBM)
PARAMS = pltpu.CompilerParams(vmem_limit_bytes=VMEM_LIMIT)


def call(kernel, in_specs, outs, scratch):
    return pl.pallas_call(
        kernel,
        out_shape=outs,
        in_specs=in_specs,
        out_specs=[VM] * len(outs),
        scratch_shapes=scratch,
        compiler_params=PARAMS,
    )


CELL = struct(32, 8, 128)


def scratch_for(last):
    shared = [
        pltpu.VMEM((4, 256, 128), F32),
        pltpu.VMEM((320, 128), F32),
        pltpu.VMEM((32, 8, 128), F32),
        pltpu.VMEM((32, 8, 128), F32),
    ]
    return shared + [pltpu.VMEM((8, 32, 128), F32) if last else pltpu.VMEM((2, 8, 128), F32)]


FORCING = [
    pltpu.VMEM((256, 256), BF16),
    pltpu.VMEM((2, 8, 32, 128), F32),
]
BORDERS = [struct(32, 2, 8, 128), struct(32, 2, 8, 128), struct(8, 128), struct(8, 128)]


def shifts(axis):
    count = lax.axis_size(axis)
    up = [(i, (i + 1) % count) for i in range(count)]
    return up, [(j, i) for i, j in up]


def swap_rows(row_low, row_high):
    up, down = shifts("rows")
    return lax.ppermute(row_high, "rows", up), lax.ppermute(row_low, "rows", down)


def swap_all(low, high, row_low, row_high):
    up, down = shifts("cols")
    return lax.ppermute(high, "cols", up), lax.ppermute(low, "cols", down), *swap_rows(row_low, row_high)


def swap_waves(near, far, row_low, row_high):
    count = lax.axis_size("cols")
    near_pairs = [(i, i ^ 1) for i in range(count)]
    far_pairs = [(i, (i - 1 if i % 2 == 0 else i + 1) % count) for i in range(count)]
    got = lax.ppermute(near, "cols", near_pairs), lax.ppermute(far, "cols", far_pairs)
    return *got, *swap_rows(row_low, row_high)


def everywhere(x):
    x = jnp.sum(lax.all_to_all(x, "rows", 0, 0), axis=0)
    x = jnp.broadcast_to(x[None], (lax.axis_size("cols"),) + x.shape)
    return jnp.sum(lax.all_to_all(x, "cols", 0, 0), axis=0)


def local(forcing, material, capacity_table, conductance_table, sink_table):
    steps = forcing.shape[0]
    n_cols, n_rows = lax.axis_size("cols"), lax.axis_size("rows")
    sizes = (16 * n_cols, 1024 * n_rows)
    cap, con, sink, *facing = call(
        materials_kernel,
        [HBM] * 2,
        [CELL, struct(256, 128), CELL] + [struct(2, 8, 128)] * 2 + [struct(4, 8, 128)] * 2,
        [pltpu.VMEM((8, 32, 128), F32)]
        + [pltpu.SMEM((3, 8), F32), pltpu.VMEM(material.shape, jnp.int32), pltpu.SemaphoreType.DMA((2,))],
    )(jnp.stack([capacity_table, conductance_table, sink_table]), material)
    con_low, con_high, row_low, row_high = swap_all(*facing)
    column = lax.axis_index("cols") * 16 + jnp.arange(16, dtype=jnp.int32)
    row = lax.axis_index("rows") * 1024 + jnp.arange(1024, dtype=jnp.int32)
    power = column.astype(F32)[:, None] / float(sizes[0]) + row.astype(F32)[None, :] / float(sizes[1])
    source = forcing * jnp.power(jnp.float32(3.0), power)
    co, sums, final, squares, *borders = call(
        functools.partial(sweep_kernel, True, False, sizes),
        [VM] * 8,
        [struct(len(KEYS), 8, 128), CELL, CELL, struct(8, 128)] + BORDERS,
        scratch_for(False) + FORCING,
    )(cap, con, sink, con_low, con_high, row_low, row_high, source)
    sums, final, squares, *borders = call(
        functools.partial(sweep_kernel, False, False, sizes),
        [VM] * 8,
        [CELL, CELL, struct(8, 128)] + BORDERS,
        scratch_for(False),
    )(co, sums, final, squares, *swap_waves(*borders))
    start, mean, squares = call(
        functools.partial(sweep_kernel, False, True, sizes),
        [VM] * 8,
        [struct(2, 16, 1024), struct(2, 16, 1024), struct(n_rows, 1, 128)],
        scratch_for(True),
    )(co, sums, final, squares, *swap_waves(*borders))
    summed = everywhere(squares)[0, :SWEEPS]
    count = float(steps * 2 * sizes[0] * sizes[1])
    return start, mean, jnp.sqrt(summed / count + 1e-06)


def solution(mesh):
    return jax.shard_map(
        local,
        mesh=mesh,
        in_specs=(P(None, None, "cols", "rows"), P(None, "cols", "rows"), P(), P(), P()),
        out_specs=(P(None, "cols", "rows"), P(None, "cols", "rows"), P()),
        check_vma=False,
    )
```

```python
import functools

import jax
import jax.numpy as jnp
from jax import lax
from jax.experimental import pallas as pl
from jax.experimental.pallas import tpu as pltpu
from jax.sharding import PartitionSpec as P

PASSES = 8
SWEEPS = 3
STEPS = 32
HALF = 16
F32 = jnp.float32
BF16 = jnp.bfloat16
VMEM_LIMIT = 24 * 2**20

CELLS = [(a, h, j) for a in range(2) for h in range(2) for j in range(8)]
GHOSTS = [(a, h, j) for a in range(2) for h in range(2) for j in (-1, 8)]
WIDE = CELLS + GHOSTS
CP, CM, RP, RM, VV = range(5)


def home(p):
    return (p[0], p[1], p[2] % 8)


def colour(p):
    return sum(p) % 2


UNIT = set()
for _a in range(2):
    for _h in range(2):
        for _j in range(8):
            if _j > 3:
                UNIT.add((RM, (_a, _h, _j)))
            if _j < 3:
                UNIT.add((RP, (_a, _h, _j)))
    UNIT.add((CM, (_a, 1, 3)))
UNIT.add((VV, (1, 0, 3)))

AT = {p: i for i, p in enumerate(WIDE)}
CELLS_SET = frozenset(CELLS)
KEYS = [("w", d, p) for p in WIDE for d in range(5) if (d, home(p)) not in UNIT]
KEYS += [("e", 0, p) for p in WIDE]
KEYS += [("alpha", 0, p) for p in CELLS]
KEYS += [("cap", 0, p) for p in CELLS]
KEYS += [("g", 0, p) for p in CELLS]
KEYS += [("oc", side, a) for side in range(2) for a in range(2)]
KEYS += [("or", side, q) for side in range(2) for q in range(4)]
COEF = {k: i for i, k in enumerate(KEYS)}


def lanes():
    return lax.broadcasted_iota(jnp.int32, (8, 128), 1)


def sublanes():
    return lax.broadcasted_iota(jnp.int32, (8, 128), 0)


def neighbour(x, p, d, cache):
    a, h, j = p

    def turned(source, shift):
        key = (source, shift)
        if key not in cache:
            cache[key] = pltpu.roll(x[source], shift, 0)
        return cache[key]

    if d == VV:
        return x[(1 - a, h, j)]
    if d == CP:
        return x[(a, 1, j)] if h == 0 else turned((a, 0, j), 7)
    if d == CM:
        return x[(a, 0, j)] if h == 1 else turned((a, 1, j), 1)
    return x[(a, h, j + 1)] if d == RP else x[(a, h, j - 1)]


def permutation(to_cells):
    first = lax.broadcasted_iota(jnp.int32, (256, 256), 0)
    second = lax.broadcasted_iota(jnp.int32, (256, 256), 1)
    row, spot = (first, second) if to_cells else (second, first)
    return jnp.where(row == 8 * (spot % 32) + spot // 32, 1.0, 0.0).astype(BF16)


def permute(x, matrix):
    high = x.astype(BF16)
    low = (x - high.astype(F32)).astype(BF16)
    both = jnp.dot(jnp.concatenate([high, low], axis=0), matrix, preferred_element_type=F32)
    return both[: x.shape[0]] + both[x.shape[0] :]


def materials_kernel(*refs):
    (tables_in, material_in, cap_o, con_o, sink_o, low_o, high_o, row_low_o, row_high_o, held, tables, material) = refs[:12]
    arrived = refs[12]
    copies = [
        pltpu.make_async_copy(tables_in, tables, arrived.at[0]),
        pltpu.make_async_copy(material_in, material, arrived.at[1]),
    ]
    for copy in copies:
        copy.start()
    for copy in copies:
        copy.wait()
    kinds = material[...].reshape(32, 1024).astype(F32).astype(BF16)
    matrix = permutation(True)
    for t in range(4):
        moved = jnp.dot(kinds[:, t * 256 : (t + 1) * 256], matrix, preferred_element_type=F32)
        for j in range(8):
            held[j, :, t * 32 : (t + 1) * 32] = moved[:, j * 32 : (j + 1) * 32]
    for p in CELLS:
        a, h, j = p
        kind = held[j, pl.ds(a * 16 + h, 8, stride=2), :]
        values = [jnp.full((8, 128), tables[t, 0], F32) for t in range(3)]
        for m in range(1, 8):
            hit = kind > m - 0.5
            values = [jnp.where(hit, tables[t, m], v) for t, v in enumerate(values)]
        i = AT[p]
        cap_o[i], con_o[pl.ds(i * 8, 8), :], sink_o[i] = values
        if j == 0:
            row_low_o[a * 2 + h] = values[1]
        if j == 7:
            row_high_o[a * 2 + h] = values[1]
    for a in range(2):
        low_o[a] = con_o[pl.ds(a * 128, 8, stride=8), :]
        high_o[a] = con_o[pl.ds(a * 128 + 64 + 7, 8, stride=8), :]


def bring(step, matrix):
    pieces = []
    for t in range(4):
        x = step[:, :, t * 256 : (t + 1) * 256].reshape(32, 256)
        high = x.astype(BF16)
        pieces += [high, (x - high.astype(F32)).astype(BF16)]
    both = jnp.dot(jnp.concatenate(pieces, axis=0), matrix, preferred_element_type=F32)
    return [both[t * 64 : t * 64 + 32] + both[t * 64 + 32 : t * 64 + 64] for t in range(4)]


def coefficients(place, sizes, cap, con, sink, con_low, con_high, row_low, row_high, co):
    n_cols, n_rows = sizes
    k = {p: con[pl.ds(AT[p] * 8, 8), :] for p in CELLS}
    row_at, col_at = place
    one, none = jnp.float32(1.0), jnp.float32(0.0)
    has_left = jnp.where(col_at > 0, one, none)
    has_right = jnp.where(col_at < n_cols // 16 - 1, one, none)
    has_before = jnp.where(row_at > 0, one, none)
    has_after = jnp.where(row_at < n_rows // 1024 - 1, one, none)
    edge_in = {}
    edge_out = {}
    lane, sub = lanes(), sublanes()

    def couple(x, y):
        return 2.0 * x * y / (x + y)

    weight = {}
    inverse = {}
    for p in CELLS:
        a, h, j = p
        q = a * 2 + h
        others = []
        if h == 0:
            others.append((k[(a, 1, j)], None))
            left = jnp.broadcast_to(con_low[a, pl.ds(j, 1), :], (8, 128)) * has_left
            others.append((jnp.where(sub == 0, left, pltpu.roll(k[(a, 1, j)], 1, 0)), sub == 0))
        else:
            right = jnp.broadcast_to(con_high[a, pl.ds(j, 1), :], (8, 128)) * has_right
            others.append((jnp.where(sub == 7, right, pltpu.roll(k[(a, 0, j)], 7, 0)), sub == 7))
            others.append((k[(a, 0, j)], None))
        if j < 7:
            others.append((k[(a, h, j + 1)], None))
        else:
            after = jnp.where(lane == 127, pltpu.roll(row_high[q], 127, 1) * has_after, pltpu.roll(k[(a, h, 0)], 127, 1))
            others.append((after, lane == 127))
        if j > 0:
            others.append((k[(a, h, j - 1)], None))
        else:
            before = jnp.where(lane == 0, pltpu.roll(row_low[q], 1, 1) * has_before, pltpu.roll(k[(a, h, 7)], 1, 1))
            others.append((before, lane == 0))
        others.append((k[(1 - a, h, j)], None))
        edges = [couple(k[p], other) for other, _ in others]
        capacity = cap[AT[p]]
        diagonal = capacity + sink[AT[p]]
        for e in edges:
            diagonal = diagonal + e
        inverse[p] = 1.0 / diagonal
        for d, (e, (_, mask)) in enumerate(zip(edges, others)):
            e = e * inverse[p]
            edge_in[d, p] = e if mask is None else jnp.where(mask, 0.0, e)
            edge_out[d, p] = None if mask is None else jnp.where(mask, e, 0.0)
    alpha = {(0, 0, 3): jnp.ones((8, 128), F32)}
    alpha[(1, 0, 3)] = edge_in[VV, (1, 0, 3)] * alpha[(0, 0, 3)]
    for a in range(2):
        alpha[(a, 1, 3)] = edge_in[CM, (a, 1, 3)] * alpha[(a, 0, 3)]
        for h in range(2):
            for j in range(4, 8):
                alpha[(a, h, j)] = edge_in[RM, (a, h, j)] * alpha[(a, h, j - 1)]
            for j in (2, 1, 0):
                alpha[(a, h, j)] = edge_in[RP, (a, h, j)] * alpha[(a, h, j + 1)]
    for a in range(2):
        for h in range(2):
            alpha[(a, h, -1)] = pltpu.roll(alpha[(a, h, 7)], 1, 1)
            alpha[(a, h, 8)] = pltpu.roll(alpha[(a, h, 0)], 127, 1)

    def put(kind, d, p, value):
        co[COEF[(kind, d, p)]] = value

    cache = {}
    scaled_out = {}
    for p in CELLS:
        a, h, j = p
        over = 1.0 / alpha[p]
        put("alpha", 0, p, alpha[p])
        put("cap", 0, p, cap[AT[p]] * alpha[p])
        e = cap[AT[p]] * inverse[p] - 1.0
        put("e", 0, p, e)
        put("g", 0, p, inverse[p] * over)
        if j == 7:
            put("e", 0, (a, h, -1), pltpu.roll(e, 1, 1))
        if j == 0:
            put("e", 0, (a, h, 8), pltpu.roll(e, 127, 1))
        for d in range(5):
            if edge_out[d, p] is not None:
                scaled_out[d, p] = edge_out[d, p] * over
            if (d, p) in UNIT:
                continue
            w = edge_in[d, p] * neighbour(alpha, p, d, cache) * over
            put("w", d, p, w)
            if j == 7:
                put("w", d, (a, h, -1), pltpu.roll(w, 1, 1))
            if j == 0:
                put("w", d, (a, h, 8), pltpu.roll(w, 127, 1))
    for a in range(2):
        low, high = jnp.zeros((8, 128), F32), jnp.zeros((8, 128), F32)
        for j in range(8):
            low = jnp.where(sub == j, jnp.broadcast_to(scaled_out[CM, (a, 0, j)][0:1], (8, 128)), low)
            high = jnp.where(sub == j, jnp.broadcast_to(scaled_out[CP, (a, 1, j)][7:8], (8, 128)), high)
        put("oc", 0, a, low)
        put("oc", 1, a, high)
        for h in range(2):
            put("or", 0, a * 2 + h, scaled_out[RM, (a, h, 0)])
            put("or", 1, a * 2 + h, scaled_out[RP, (a, h, 7)])


SKEW = True


def rows_of(p):
    return pl.ds(AT[p] * 8, 8)


def time_step(source, extra, co, held):
    def applied(x, p, cache, memo):
        total = None
        for d in (VV, CP, CM, RP, RM):
            term = neighbour(x, p, d, cache)
            if (d, home(p)) not in UNIT:
                if d not in memo:
                    memo[d] = co[COEF[("w", d, p)]]
                term = memo[d] * term
            total = term if total is None else total + term
        return total

    def add_ghosts(x):
        for a, h, j in list(x):
            if j >= 6:
                x[(a, h, j - 8)] = pltpu.roll(x[(a, h, j)], 1, 1)
            if j <= 1:
                x[(a, h, j + 8)] = pltpu.roll(x[(a, h, j)], 127, 1)

    start = [{p: held[0][rows_of(p), :] for p in CELLS if colour(p) == c} for c in range(2)]
    for c in range(2):
        add_ghosts(start[c])
    fields = [dict(start[0]), dict(start[1])]
    lag = 1 if SKEW else 0
    for stage in range(1, PASSES + 1 + lag):
        jobs = []
        for chain in (1, 0):
            k = stage - chain * lag
            if 1 <= k <= PASSES:
                wide = k % 2 == 1
                if wide and k > 1:
                    add_ghosts(fields[chain])
                jobs.append((chain, k, wide, (chain + k) % 2, {}, {}))
        memos = {}
        for p in WIDE:
            for chain, k, wide, to, cache, out in jobs:
                if colour(p) != to or (not wide and p not in CELLS_SET):
                    continue
                value = applied(fields[chain], p, cache, memos.setdefault(p, {}))
                if k == 1:
                    base = source(p) + co[COEF[("e", 0, p)]] * start[to][p]
                    if extra is not None and p in extra:
                        base = base + extra[p]
                    value = value + base
                elif k == 2:
                    value = value + held[1][rows_of(p), :]
                elif k == 4:
                    value = value + held[2][rows_of(p), :]
                elif k == 8:
                    value = value + (held[3][rows_of(p), :] + held[0][rows_of(p), :])
                if k == 1 and p in CELLS_SET:
                    held[1][rows_of(p), :] = value
                elif k in (2, 4):
                    held[k // 2 + 1][rows_of(p), :] = value
                out[p] = value
        for chain, k, wide, to, cache, out in jobs:
            fields[chain] = out
    return {**fields[0], **fields[1]}


def sweep_kernel(first, last, top, bottom, sizes, names, *refs):
    r = dict(zip(names, refs))
    whole, ends = top - bottom == STEPS - 1, bottom == 0
    co, sums, squares, f_ref, lane = r["co"], r["sums"], r["squares"], r["f"], lanes()
    if first:
        facing = [r[k] for k in ("cap", "con", "sink", "con_low", "con_high", "row_low", "row_high")]
        matrix, force, forcing = r["matrix"], r["force"], r["forcing"]
        place = (lax.axis_index("rows"), lax.axis_index("cols"))
        matrix[...] = permutation(True)
        coefficients(place, sizes, *facing, co)

        def fetch(now, slot):
            for t, block in enumerate(bring(forcing[now], matrix[...])):
                for j in range(8):
                    force[slot, j, :, t * 32 : (t + 1) * 32] = block[:, j * 32 : (j + 1) * 32]

        fetch(top, 1)
    stages = [r["fields"].at[k] for k in range(4)]
    y = stages[0]
    if top == STEPS - 1:
        y[...] = jnp.zeros_like(y)
        squares[...] = jnp.zeros_like(squares)
    else:
        y[...] = r["y_in"][...]
        squares[...] = r["squares_in"][...]
    if first:
        sums[...] = jnp.zeros_like(sums)
    else:
        sums[...] = r["sums_in"][...]
        f_ref[...] = jnp.zeros_like(f_ref)
    if not last:
        rows_ref = r["rows"]
        rows_ref[...] = jnp.zeros_like(rows_ref) if top == STEPS - 1 else r["rows_in"][...]
    even = lax.axis_index("cols") % 2 == 0
    even_row = lax.axis_index("rows") % 2 == 0

    def record(at):
        edges = r["edges"]
        for a in range(2):
            low = y[pl.ds(a * 128, 8, stride=8), :]
            high = y[pl.ds(a * 128 + 64 + 7, 8, stride=8), :]
            edges[0, at - bottom, a] = jnp.where(even, high, low)
            edges[1, at - bottom, a] = jnp.where(even, low, high)
        lows, highs = rows_ref[0], rows_ref[1]
        for q in range(4):
            a, h = q // 2, q % 2
            spot = q * 32 + at
            lows = jnp.where(lane == spot, pltpu.roll(y[rows_of((a, h, 0)), :], spot, 1), lows)
            highs = jnp.where(lane == spot, pltpu.roll(y[rows_of((a, h, 7)), :], (spot + 1) % 128, 1), highs)
        rows_ref[0] = lows
        rows_ref[1] = highs

    def one(now, slot):
        if not last:
            record(jnp.minimum(now + 1, top))
        extra = None
        if first:
            memo = {}

            def source(p):
                a, h, j = home(p)
                if (a, h, j) not in memo:
                    rows = pl.ds(a * 16 + h, 8, stride=2)
                    memo[(a, h, j)] = force[slot, j, rows, :] * co[COEF[("g", 0, (a, h, j))]]
                value = memo[(a, h, j)]
                if p[2] == -1:
                    value = pltpu.roll(value, 1, 1)
                if p[2] == 8:
                    value = pltpu.roll(value, 127, 1)
                return value

        else:
            extra = {}
            for side in range(2):
                for a in range(2):
                    near, far = r["got_near"][now - bottom, a], r["got_far"][now - bottom, a]
                    got = jnp.where(even, near, far) if side else jnp.where(even, far, near)
                    value = got * co[COEF[("oc", side, a)]]
                    base = (a * 2 + side) * 64
                    s = 7 * side
                    f_ref[pl.ds(base + s, 8, stride=8), :] = value
                    f_ref[pl.ds(AT[(a, side, -1)] * 8 + s, 1), :] = pltpu.roll(value, 1, 1)[7:8]
                    f_ref[pl.ds(AT[(a, side, 8)] * 8 + s, 1), :] = pltpu.roll(value, 127, 1)[0:1]
            row_near, row_far = r["got_row_near"][0], r["got_row_far"][0]
            row_low = jnp.where(even_row, row_far, row_near)
            row_high = jnp.where(even_row, row_near, row_far)
            for q in range(4):
                a, h = q // 2, q % 2
                spot = q * 32 + now
                extra[(a, h, 0)] = co[COEF[("or", 0, q)]] * pltpu.roll(row_low, (128 - spot) % 128, 1)
                extra[(a, h, 7)] = co[COEF[("or", 1, q)]] * pltpu.roll(row_high, 127 - spot, 1)

            def source(p):
                return f_ref[pl.ds(AT[p] * 8, 8), :]

        done = time_step(source, extra, co, stages)
        if first:
            fetch(jnp.maximum(now - 1, 0), 1 - slot)
        for p in CELLS:
            i_p = AT[p]
            x = done[p]
            y[rows_of(p), :] = x
            sums[i_p] += x
            squares[i_p] += x * x

    def body(i, carry):
        one(top - 2 * i, 1)
        one(top - 1 - 2 * i, 0)
        return carry

    lax.fori_loop(0, (top - bottom + 1) // 2, body, 0)

    def alpha(p):
        return co[COEF[("alpha", 0, p)]]

    sub = sublanes()
    if not last:
        record(bottom)
        for a in range(2):
            scale = []
            for side in range(2):
                compact = jnp.zeros((8, 128), F32)
                for j in range(8):
                    row = alpha((a, side, j))[7 * side : 7 * side + 1]
                    compact = jnp.where(sub == j, jnp.broadcast_to(row, (8, 128)), compact)
                scale.append(compact)
            near_scale = jnp.where(even, scale[1], scale[0])
            far_scale = jnp.where(even, scale[0], scale[1])
            for n in range(bottom, top + 1):
                half, k = ("upper", n - HALF) if n >= HALF else ("lower", n)
                r["near_" + half][k, a] = r["edges"][0, n - bottom, a] * near_scale
                r["far_" + half][k, a] = r["edges"][1, n - bottom, a] * far_scale
    if not ends:
        r["y_out"][...] = y[...]
        return
    total = jnp.zeros((8, 128), F32)
    for p in CELLS:
        total = total + squares[AT[p]] * (alpha(p) * alpha(p))
    total = jnp.sum(jnp.sum(total, axis=1, keepdims=True), axis=0, keepdims=True)
    spread = jnp.broadcast_to(total, (8, 128))
    if first:
        r["norms"][...] = jnp.where(lane == 0, spread, 0.0)
    else:
        spread = jnp.where(lane == (2 if last else 1), spread, r["norms_in"][...])
        if last:
            for n in range(r["norms"].shape[0]):
                r["norms"][n] = spread[0:1]
        else:
            r["norms"][...] = spread
    if not last:
        final = y[...].reshape(32, 8, 128)
        r["final"][...] = final if first else final + r["final_in"][...]
        turned = []
        for side in range(2):
            spread_row = jnp.zeros((8, 128), F32)
            for q in range(4):
                a, h = q // 2, q % 2
                one_lane = alpha((a, h, 7 * side))
                one_lane = one_lane[:, 127:128] if side else one_lane[:, 0:1]
                spread_row = jnp.where(lane // 32 == q, jnp.broadcast_to(one_lane, (8, 128)), spread_row)
            turned.append(rows_ref[side] * spread_row)
        for name, value in (("row_near", (turned[1], turned[0])), ("row_far", turned)):
            r[name][...] = jnp.zeros_like(r[name])
            r[name][0] = jnp.where(even_row, *value)
    else:
        matrix, held = permutation(False), r["held"]
        for p in CELLS:
            a, h, j = p
            i_p = AT[p]
            start = (r["final_in"][i_p] + y[rows_of(p), :]) * co[COEF[("cap", 0, p)]]
            held[j, pl.ds(a * 16 + h, 8, stride=2), :] = start
            held[j, pl.ds(32 + a * 16 + h, 8, stride=2), :] = sums[i_p] * alpha(p) * (1.0 / STEPS)
        for t in range(4):
            piece = jnp.concatenate([held[j, :, t * 32 : (t + 1) * 32] for j in range(8)], axis=1)
            moved = permute(piece, matrix).reshape(4, 16, 256)
            r["start"][:, :, t * 256 : (t + 1) * 256] = moved[:2]
            r["mean"][:, :, t * 256 : (t + 1) * 256] = moved[2:]


def struct(*shape):
    return jax.ShapeDtypeStruct(shape, F32)


VM = pl.BlockSpec(memory_space=pltpu.VMEM)
HBM = pl.BlockSpec(memory_space=pltpu.HBM)
PARAMS = pltpu.CompilerParams(vmem_limit_bytes=VMEM_LIMIT)


def call(kernel, in_specs, outs, scratch):
    return pl.pallas_call(
        kernel,
        out_shape=outs,
        in_specs=in_specs,
        out_specs=[VM] * len(outs),
        scratch_shapes=scratch,
        compiler_params=PARAMS,
    )


CELL = struct(32, 8, 128)
WAVE = struct(HALF, 2, 8, 128)
LANES = struct(8, 128)
ROWS = struct(64, 8, 128)


def run_sweep(first, last, top, bottom, sizes, inputs, outs):
    scratch = {"fields": pltpu.VMEM((4, 256, 128), F32), "f": pltpu.VMEM((320, 128), F32)}
    kept = {name: pltpu.VMEM((32, 8, 128), F32) for name in ("sums", "squares") if name not in outs}
    if not last:
        scratch["edges"] = pltpu.VMEM((2, top - bottom + 1, 2, 8, 128), F32)
        if "rows" not in outs:
            scratch["rows"] = pltpu.VMEM((2, 8, 128), F32)
    elif bottom == 0:
        scratch["held"] = pltpu.VMEM((8, 64, 128), F32)
    if first:
        scratch["matrix"] = pltpu.VMEM((256, 256), BF16)
        scratch["force"] = pltpu.VMEM((2, 8, 32, 128), F32)
    scratch = scratch | kept
    names = [*inputs, *outs, *scratch]
    kernel = functools.partial(sweep_kernel, first, last, top, bottom, sizes, names)
    got = call(kernel, [VM] * len(inputs), list(outs.values()), list(scratch.values()))(*inputs.values())
    return dict(zip(outs, got))


def shifts(axis):
    count = lax.axis_size(axis)
    up = [(i, (i + 1) % count) for i in range(count)]
    return up, [(j, i) for i, j in up]


def swap_all(low, high, row_low, row_high):
    up, down = shifts("cols")
    rows_up, rows_down = shifts("rows")
    return (
        lax.ppermute(high, "cols", up),
        lax.ppermute(low, "cols", down),
        lax.ppermute(row_high, "rows", rows_up),
        lax.ppermute(row_low, "rows", rows_down),
    )


def swap_pairs(near, far, axis):
    count = lax.axis_size(axis)
    near_pairs = [(i, i ^ 1) for i in range(count)]
    far_pairs = [(i, (i - 1 if i % 2 == 0 else i + 1) % count) for i in range(count)]
    got_far = lax.ppermute(far, axis, far_pairs)
    return lax.ppermute(near, axis, near_pairs), got_far


def swap_waves(waves):
    upper = swap_pairs(waves["near_upper"], waves["far_upper"], "cols")
    rows = swap_pairs(waves["row_near"], waves["row_far"], "rows")
    lower = swap_pairs(waves["near_lower"], waves["far_lower"], "cols")
    return upper, rows, lower


def later_sweep(last, sizes, n_rows, before, co, sums, waves):
    upper, rows, lower = swap_waves(waves)
    row_in = {"got_row_near": rows[0], "got_row_far": rows[1]}
    inputs = {"co": co, "sums_in": sums, "got_near": upper[0], "got_far": upper[1]} | row_in
    outs = {"y_out": struct(256, 128), "sums": CELL, "squares": CELL}
    if not last:
        outs |= {"rows": struct(2, 8, 128), "near_upper": WAVE, "far_upper": WAVE}
    mid = run_sweep(False, last, STEPS - 1, HALF, sizes, inputs, outs)
    inputs = {"co": co, "sums_in": mid["sums"], "squares_in": mid["squares"], "y_in": mid["y_out"]}
    inputs |= {"got_near": lower[0], "got_far": lower[1], "final_in": before["final"], "norms_in": before["norms"]}
    inputs |= row_in
    if last:
        whole = struct(2, 16, 1024)
        outs = {"start": whole, "mean": whole, "norms": struct(n_rows, 1, 128)}
    else:
        inputs["rows_in"] = mid["rows"]
        outs = {"sums": CELL, "final": CELL, "norms": LANES, "near_lower": WAVE, "far_lower": WAVE}
        outs |= {"row_near": ROWS, "row_far": ROWS}
    return mid | run_sweep(False, last, HALF - 1, 0, sizes, inputs, outs)


def everywhere(x):
    x = jnp.sum(lax.all_to_all(x, "rows", 0, 0), axis=0)
    x = jnp.broadcast_to(x[None], (lax.axis_size("cols"),) + x.shape)
    return jnp.sum(lax.all_to_all(x, "cols", 0, 0), axis=0)


def local(forcing, material, capacity_table, conductance_table, sink_table):
    steps = forcing.shape[0]
    n_cols, n_rows = lax.axis_size("cols"), lax.axis_size("rows")
    sizes = (16 * n_cols, 1024 * n_rows)
    cap, con, sink, *facing = call(
        materials_kernel,
        [HBM] * 2,
        [CELL, struct(256, 128), CELL] + [struct(2, 8, 128)] * 2 + [struct(4, 8, 128)] * 2,
        [pltpu.VMEM((8, 32, 128), F32)]
        + [pltpu.SMEM((3, 8), F32), pltpu.VMEM(material.shape, jnp.int32), pltpu.SemaphoreType.DMA((2,))],
    )(jnp.stack([capacity_table, conductance_table, sink_table]), material)
    con_low, con_high, row_low, row_high = swap_all(*facing)
    column = lax.axis_index("cols") * 16 + jnp.arange(16, dtype=jnp.int32)
    row = lax.axis_index("rows") * 1024 + jnp.arange(1024, dtype=jnp.int32)
    power = column.astype(F32)[:, None] / float(sizes[0]) + row.astype(F32)[None, :] / float(sizes[1])
    source = forcing * jnp.power(jnp.float32(3.0), power)
    inputs = {"cap": cap, "con": con, "sink": sink, "con_low": con_low, "con_high": con_high}
    inputs |= {"row_low": row_low, "row_high": row_high, "forcing": source}
    outs = {"co": struct(len(KEYS), 8, 128), "sums": CELL, "final": CELL, "norms": LANES}
    outs |= {name: WAVE for name in ("near_upper", "far_upper", "near_lower", "far_lower")}
    outs |= {"row_near": ROWS, "row_far": ROWS}
    one = run_sweep(True, False, STEPS - 1, 0, sizes, inputs, outs)
    two = later_sweep(False, sizes, n_rows, one, one["co"], one["sums"], one)
    three = later_sweep(True, sizes, n_rows, two, one["co"], two["sums"], two)
    start, mean = three["start"], three["mean"]
    summed = everywhere(three["norms"])[0, :SWEEPS]
    count = float(steps * 2 * sizes[0] * sizes[1])
    return start, mean, jnp.sqrt(summed / count + 1e-06)


def solution(mesh):
    return jax.shard_map(
        local,
        mesh=mesh,
        in_specs=(P(None, None, "cols", "rows"), P(None, "cols", "rows"), P(), P(), P()),
        out_specs=(P(None, "cols", "rows"), P(None, "cols", "rows"), P()),
        check_vma=False,
    )
```

```python
import functools

import jax
import jax.numpy as jnp
from jax import lax
from jax.experimental import pallas as pl
from jax.experimental.pallas import tpu as pltpu
from jax.sharding import PartitionSpec as P

PASSES = 8
SWEEPS = 3
STEPS = 32
HALF = 16
F32 = jnp.float32
BF16 = jnp.bfloat16
VMEM_LIMIT = 24 * 2**20

CELLS = [(a, h, j) for a in range(2) for h in range(2) for j in range(8)]
GHOSTS = [(a, h, j) for a in range(2) for h in range(2) for j in (-1, 8)]
WIDE = CELLS + GHOSTS
CP, CM, RP, RM, VV = range(5)


def home(p):
    return (p[0], p[1], p[2] % 8)


def colour(p):
    return sum(p) % 2


UNIT = set()
for _a in range(2):
    for _h in range(2):
        for _j in range(8):
            if _j > 3:
                UNIT.add((RM, (_a, _h, _j)))
            if _j < 3:
                UNIT.add((RP, (_a, _h, _j)))
    UNIT.add((CM, (_a, 1, 3)))
UNIT.add((VV, (1, 0, 3)))

AT = {p: i for i, p in enumerate(WIDE)}
CELLS_SET = frozenset(CELLS)
KEYS = [("w", d, p) for p in WIDE for d in range(5) if (d, home(p)) not in UNIT]
KEYS += [("e", 0, p) for p in WIDE]
KEYS += [("alpha", 0, p) for p in CELLS]
KEYS += [("cap", 0, p) for p in CELLS]
KEYS += [("g", 0, p) for p in CELLS]
KEYS += [("oc", side, a) for side in range(2) for a in range(2)]
KEYS += [("or", side, q) for side in range(2) for q in range(4)]
COEF = {k: i for i, k in enumerate(KEYS)}


def lanes():
    return lax.broadcasted_iota(jnp.int32, (8, 128), 1)


def sublanes():
    return lax.broadcasted_iota(jnp.int32, (8, 128), 0)


def neighbour(x, p, d, cache):
    a, h, j = p

    def turned(source, shift):
        key = (source, shift)
        if key not in cache:
            cache[key] = pltpu.roll(x[source], shift, 0)
        return cache[key]

    if d == VV:
        return x[(1 - a, h, j)]
    if d == CP:
        return x[(a, 1, j)] if h == 0 else turned((a, 0, j), 7)
    if d == CM:
        return x[(a, 0, j)] if h == 1 else turned((a, 1, j), 1)
    return x[(a, h, j + 1)] if d == RP else x[(a, h, j - 1)]


def permutation(to_cells):
    first = lax.broadcasted_iota(jnp.int32, (256, 256), 0)
    second = lax.broadcasted_iota(jnp.int32, (256, 256), 1)
    row, spot = (first, second) if to_cells else (second, first)
    return jnp.where(row == 8 * (spot % 32) + spot // 32, 1.0, 0.0).astype(BF16)


def permute(x, matrix):
    high = x.astype(BF16)
    low = (x - high.astype(F32)).astype(BF16)
    both = jnp.dot(jnp.concatenate([high, low], axis=0), matrix, preferred_element_type=F32)
    return both[: x.shape[0]] + both[x.shape[0] :]


def materials_kernel(*refs):
    (tables_in, material_in, cap_o, con_o, sink_o, low_o, high_o, row_low_o, row_high_o, held, tables, material) = refs[:12]
    arrived = refs[12]
    copies = [
        pltpu.make_async_copy(tables_in, tables, arrived.at[0]),
        pltpu.make_async_copy(material_in, material, arrived.at[1]),
    ]
    for copy in copies:
        copy.start()
    for copy in copies:
        copy.wait()
    kinds = material[...].reshape(32, 1024).astype(F32).astype(BF16)
    matrix = permutation(True)
    for t in range(4):
        moved = jnp.dot(kinds[:, t * 256 : (t + 1) * 256], matrix, preferred_element_type=F32)
        for j in range(8):
            held[j, :, t * 32 : (t + 1) * 32] = moved[:, j * 32 : (j + 1) * 32]
    for p in CELLS:
        a, h, j = p
        kind = held[j, pl.ds(a * 16 + h, 8, stride=2), :]
        values = [jnp.full((8, 128), tables[t, 0], F32) for t in range(3)]
        for m in range(1, 8):
            hit = kind > m - 0.5
            values = [jnp.where(hit, tables[t, m], v) for t, v in enumerate(values)]
        i = AT[p]
        cap_o[i], con_o[pl.ds(i * 8, 8), :], sink_o[i] = values
        if j == 0:
            row_low_o[a * 2 + h] = values[1]
        if j == 7:
            row_high_o[a * 2 + h] = values[1]
    for a in range(2):
        low_o[a] = con_o[pl.ds(a * 128, 8, stride=8), :]
        high_o[a] = con_o[pl.ds(a * 128 + 64 + 7, 8, stride=8), :]


def bring(step, matrix):
    pieces = []
    for t in range(4):
        x = step[:, :, t * 256 : (t + 1) * 256].reshape(32, 256)
        high = x.astype(BF16)
        pieces += [high, (x - high.astype(F32)).astype(BF16)]
    both = jnp.dot(jnp.concatenate(pieces, axis=0), matrix, preferred_element_type=F32)
    return [both[t * 64 : t * 64 + 32] + both[t * 64 + 32 : t * 64 + 64] for t in range(4)]


def coefficients(place, sizes, cap, con, sink, con_low, con_high, row_low, row_high, co):
    n_cols, n_rows = sizes
    k = {p: con[pl.ds(AT[p] * 8, 8), :] for p in CELLS}
    row_at, col_at = place
    one, none = jnp.float32(1.0), jnp.float32(0.0)
    has_left = jnp.where(col_at > 0, one, none)
    has_right = jnp.where(col_at < n_cols // 16 - 1, one, none)
    has_before = jnp.where(row_at > 0, one, none)
    has_after = jnp.where(row_at < n_rows // 1024 - 1, one, none)
    edge_in = {}
    edge_out = {}
    lane, sub = lanes(), sublanes()

    def couple(x, y):
        return 2.0 * x * y / (x + y)

    weight = {}
    inverse = {}
    for p in CELLS:
        a, h, j = p
        q = a * 2 + h
        others = []
        if h == 0:
            others.append((k[(a, 1, j)], None))
            left = jnp.broadcast_to(con_low[a, pl.ds(j, 1), :], (8, 128)) * has_left
            others.append((jnp.where(sub == 0, left, pltpu.roll(k[(a, 1, j)], 1, 0)), sub == 0))
        else:
            right = jnp.broadcast_to(con_high[a, pl.ds(j, 1), :], (8, 128)) * has_right
            others.append((jnp.where(sub == 7, right, pltpu.roll(k[(a, 0, j)], 7, 0)), sub == 7))
            others.append((k[(a, 0, j)], None))
        if j < 7:
            others.append((k[(a, h, j + 1)], None))
        else:
            after = jnp.where(lane == 127, pltpu.roll(row_high[q], 127, 1) * has_after, pltpu.roll(k[(a, h, 0)], 127, 1))
            others.append((after, lane == 127))
        if j > 0:
            others.append((k[(a, h, j - 1)], None))
        else:
            before = jnp.where(lane == 0, pltpu.roll(row_low[q], 1, 1) * has_before, pltpu.roll(k[(a, h, 7)], 1, 1))
            others.append((before, lane == 0))
        others.append((k[(1 - a, h, j)], None))
        edges = [couple(k[p], other) for other, _ in others]
        capacity = cap[AT[p]]
        diagonal = capacity + sink[AT[p]]
        for e in edges:
            diagonal = diagonal + e
        inverse[p] = 1.0 / diagonal
        for d, (e, (_, mask)) in enumerate(zip(edges, others)):
            e = e * inverse[p]
            edge_in[d, p] = e if mask is None else jnp.where(mask, 0.0, e)
            edge_out[d, p] = None if mask is None else jnp.where(mask, e, 0.0)
    alpha = {(0, 0, 3): jnp.ones((8, 128), F32)}
    alpha[(1, 0, 3)] = edge_in[VV, (1, 0, 3)] * alpha[(0, 0, 3)]
    for a in range(2):
        alpha[(a, 1, 3)] = edge_in[CM, (a, 1, 3)] * alpha[(a, 0, 3)]
        for h in range(2):
            for j in range(4, 8):
                alpha[(a, h, j)] = edge_in[RM, (a, h, j)] * alpha[(a, h, j - 1)]
            for j in (2, 1, 0):
                alpha[(a, h, j)] = edge_in[RP, (a, h, j)] * alpha[(a, h, j + 1)]
    for a in range(2):
        for h in range(2):
            alpha[(a, h, -1)] = pltpu.roll(alpha[(a, h, 7)], 1, 1)
            alpha[(a, h, 8)] = pltpu.roll(alpha[(a, h, 0)], 127, 1)

    def put(kind, d, p, value):
        co[COEF[(kind, d, p)]] = value

    cache = {}
    scaled_out = {}
    for p in CELLS:
        a, h, j = p
        over = 1.0 / alpha[p]
        put("alpha", 0, p, alpha[p])
        put("cap", 0, p, cap[AT[p]] * alpha[p])
        e = cap[AT[p]] * inverse[p] - 1.0
        put("e", 0, p, e)
        put("g", 0, p, inverse[p] * over)
        if j == 7:
            put("e", 0, (a, h, -1), pltpu.roll(e, 1, 1))
        if j == 0:
            put("e", 0, (a, h, 8), pltpu.roll(e, 127, 1))
        for d in range(5):
            if edge_out[d, p] is not None:
                scaled_out[d, p] = edge_out[d, p] * over
            if (d, p) in UNIT:
                continue
            w = edge_in[d, p] * neighbour(alpha, p, d, cache) * over
            put("w", d, p, w)
            if j == 7:
                put("w", d, (a, h, -1), pltpu.roll(w, 1, 1))
            if j == 0:
                put("w", d, (a, h, 8), pltpu.roll(w, 127, 1))
    for a in range(2):
        low, high = jnp.zeros((8, 128), F32), jnp.zeros((8, 128), F32)
        for j in range(8):
            low = jnp.where(sub == j, jnp.broadcast_to(scaled_out[CM, (a, 0, j)][0:1], (8, 128)), low)
            high = jnp.where(sub == j, jnp.broadcast_to(scaled_out[CP, (a, 1, j)][7:8], (8, 128)), high)
        put("oc", 0, a, low)
        put("oc", 1, a, high)
        for h in range(2):
            put("or", 0, a * 2 + h, scaled_out[RM, (a, h, 0)])
            put("or", 1, a * 2 + h, scaled_out[RP, (a, h, 7)])


SKEW = True


def rows_of(p):
    return pl.ds(AT[p] * 8, 8)


def time_step(source, extra, co, held):
    def applied(x, p, cache, memo):
        total = None
        for d in (VV, CP, CM, RP, RM):
            term = neighbour(x, p, d, cache)
            if (d, home(p)) not in UNIT:
                if d not in memo:
                    memo[d] = co[COEF[("w", d, p)]]
                term = memo[d] * term
            total = term if total is None else total + term
        return total

    def add_ghosts(x):
        for a, h, j in list(x):
            if j >= 6:
                x[(a, h, j - 8)] = pltpu.roll(x[(a, h, j)], 1, 1)
            if j <= 1:
                x[(a, h, j + 8)] = pltpu.roll(x[(a, h, j)], 127, 1)

    start = [{p: held[0][rows_of(p), :] for p in CELLS if colour(p) == c} for c in range(2)]
    for c in range(2):
        add_ghosts(start[c])
    fields = [dict(start[0]), dict(start[1])]
    lag = 1 if SKEW else 0
    for stage in range(1, PASSES + 1 + lag):
        jobs = []
        for chain in (1, 0):
            k = stage - chain * lag
            if 1 <= k <= PASSES:
                wide = k % 2 == 1
                if wide and k > 1:
                    add_ghosts(fields[chain])
                jobs.append((chain, k, wide, (chain + k) % 2, {}, {}))
        memos = {}
        for p in WIDE:
            for chain, k, wide, to, cache, out in jobs:
                if colour(p) != to or (not wide and p not in CELLS_SET):
                    continue
                value = applied(fields[chain], p, cache, memos.setdefault(p, {}))
                if k == 1:
                    base = source(p) + co[COEF[("e", 0, p)]] * start[to][p]
                    if extra is not None and p in extra:
                        base = base + extra[p]
                    value = value + base
                elif k == 2:
                    value = value + held[1][rows_of(p), :]
                elif k == 4:
                    value = value + held[2][rows_of(p), :]
                elif k == 8:
                    value = value + (held[3][rows_of(p), :] + held[0][rows_of(p), :])
                if k == 1 and p in CELLS_SET:
                    held[1][rows_of(p), :] = value
                elif k in (2, 4):
                    held[k // 2 + 1][rows_of(p), :] = value
                out[p] = value
        for chain, k, wide, to, cache, out in jobs:
            fields[chain] = out
    return {**fields[0], **fields[1]}


def sweep_kernel(first, last, top, bottom, sizes, names, *refs):
    r = dict(zip(names, refs))
    whole, ends = top - bottom == STEPS - 1, bottom == 0
    co, sums, squares, f_ref, lane = r["co"], r["sums"], r["squares"], r["f"], lanes()
    if first:
        facing = [r[k] for k in ("cap", "con", "sink", "con_low", "con_high", "row_low", "row_high")]
        matrix, force, forcing = r["matrix"], r["force"], r["forcing"]
        place = (lax.axis_index("rows"), lax.axis_index("cols"))
        matrix[...] = permutation(True)
        coefficients(place, sizes, *facing, co)

        def fetch(now, slot):
            for t, block in enumerate(bring(forcing[now], matrix[...])):
                for j in range(8):
                    force[slot, j, :, t * 32 : (t + 1) * 32] = block[:, j * 32 : (j + 1) * 32]

        fetch(top, 1)
    stages = [r["fields"].at[k] for k in range(4)]
    y = stages[0]
    if top == STEPS - 1:
        y[...] = jnp.zeros_like(y)
        squares[...] = jnp.zeros_like(squares)
    else:
        y[...] = r["y_in"][...]
        squares[...] = r["squares_in"][...]
    if first:
        sums[...] = jnp.zeros_like(sums)
    else:
        sums[...] = r["sums_in"][...]
        f_ref[...] = jnp.zeros_like(f_ref)
    if not last:
        rows_ref = r["rows"]
        rows_ref[...] = jnp.zeros_like(rows_ref) if top == STEPS - 1 else r["rows_in"][...]
    even = lax.axis_index("cols") % 2 == 0
    even_row = lax.axis_index("rows") % 2 == 0

    def record(at):
        edges = r["edges"]
        for a in range(2):
            low = y[pl.ds(a * 128, 8, stride=8), :]
            high = y[pl.ds(a * 128 + 64 + 7, 8, stride=8), :]
            edges[0, at - bottom, a] = jnp.where(even, high, low)
            edges[1, at - bottom, a] = jnp.where(even, low, high)
        lows, highs = rows_ref[0], rows_ref[1]
        for q in range(4):
            a, h = q // 2, q % 2
            spot = q * 32 + at
            lows = jnp.where(lane == spot, pltpu.roll(y[rows_of((a, h, 0)), :], spot, 1), lows)
            highs = jnp.where(lane == spot, pltpu.roll(y[rows_of((a, h, 7)), :], (spot + 1) % 128, 1), highs)
        rows_ref[0] = lows
        rows_ref[1] = highs

    def one(now, slot):
        if not last:
            record(jnp.minimum(now + 1, top))
        extra = None
        if first:
            memo = {}

            def source(p):
                a, h, j = home(p)
                if (a, h, j) not in memo:
                    rows = pl.ds(a * 16 + h, 8, stride=2)
                    memo[(a, h, j)] = force[slot, j, rows, :] * co[COEF[("g", 0, (a, h, j))]]
                value = memo[(a, h, j)]
                if p[2] == -1:
                    value = pltpu.roll(value, 1, 1)
                if p[2] == 8:
                    value = pltpu.roll(value, 127, 1)
                return value

        else:
            extra = {}
            for side in range(2):
                for a in range(2):
                    near, far = r["got_near"][now - bottom, a], r["got_far"][now - bottom, a]
                    got = jnp.where(even, near, far) if side else jnp.where(even, far, near)
                    value = got * co[COEF[("oc", side, a)]]
                    base = (a * 2 + side) * 64
                    s = 7 * side
                    f_ref[pl.ds(base + s, 8, stride=8), :] = value
                    f_ref[pl.ds(AT[(a, side, -1)] * 8 + s, 1), :] = pltpu.roll(value, 1, 1)[7:8]
                    f_ref[pl.ds(AT[(a, side, 8)] * 8 + s, 1), :] = pltpu.roll(value, 127, 1)[0:1]
            row_near, row_far = r["got_row_near"][0], r["got_row_far"][0]
            row_low = jnp.where(even_row, row_far, row_near)
            row_high = jnp.where(even_row, row_near, row_far)
            for q in range(4):
                a, h = q // 2, q % 2
                spot = q * 32 + now
                extra[(a, h, 0)] = co[COEF[("or", 0, q)]] * pltpu.roll(row_low, (128 - spot) % 128, 1)
                extra[(a, h, 7)] = co[COEF[("or", 1, q)]] * pltpu.roll(row_high, 127 - spot, 1)

            def source(p):
                return f_ref[pl.ds(AT[p] * 8, 8), :]

        done = time_step(source, extra, co, stages)
        if first:
            fetch(jnp.maximum(now - 1, 0), 1 - slot)
        for p in CELLS:
            i_p = AT[p]
            x = done[p]
            y[rows_of(p), :] = x
            sums[i_p] += x
            squares[i_p] += x * x

    def body(i, carry):
        one(top - 2 * i, 1)
        one(top - 1 - 2 * i, 0)
        return carry

    lax.fori_loop(0, (top - bottom + 1) // 2, body, 0)

    def alpha(p):
        return co[COEF[("alpha", 0, p)]]

    sub = sublanes()
    if not last:
        record(bottom)
        for a in range(2):
            scale = []
            for side in range(2):
                compact = jnp.zeros((8, 128), F32)
                for j in range(8):
                    row = alpha((a, side, j))[7 * side : 7 * side + 1]
                    compact = jnp.where(sub == j, jnp.broadcast_to(row, (8, 128)), compact)
                scale.append(compact)
            near_scale = jnp.where(even, scale[1], scale[0])
            far_scale = jnp.where(even, scale[0], scale[1])
            for n in range(bottom, top + 1):
                half, k = ("upper", n - HALF) if n >= HALF else ("lower", n)
                r["near_" + half][k, a] = r["edges"][0, n - bottom, a] * near_scale
                r["far_" + half][k, a] = r["edges"][1, n - bottom, a] * far_scale
    if not ends:
        r["y_out"][...] = y[...]
        return
    total = jnp.zeros((8, 128), F32)
    for p in CELLS:
        total = total + squares[AT[p]] * (alpha(p) * alpha(p))
    total = jnp.sum(jnp.sum(total, axis=1, keepdims=True), axis=0, keepdims=True)
    spread = jnp.broadcast_to(total, (8, 128))
    if first:
        r["norms"][...] = jnp.where(lane == 0, spread, 0.0)
    else:
        spread = jnp.where(lane == (2 if last else 1), spread, r["norms_in"][...])
        if last:
            for n in range(r["norms"].shape[0]):
                r["norms"][n] = spread[0:1]
        else:
            r["norms"][...] = spread
    if not last:
        final = y[...].reshape(32, 8, 128)
        r["final"][...] = final if first else final + r["final_in"][...]
        turned = []
        for side in range(2):
            spread_row = jnp.zeros((8, 128), F32)
            for q in range(4):
                a, h = q // 2, q % 2
                one_lane = alpha((a, h, 7 * side))
                one_lane = one_lane[:, 127:128] if side else one_lane[:, 0:1]
                spread_row = jnp.where(lane // 32 == q, jnp.broadcast_to(one_lane, (8, 128)), spread_row)
            turned.append(rows_ref[side] * spread_row)
        for name, value in (("row_near", (turned[1], turned[0])), ("row_far", turned)):
            r[name][...] = jnp.zeros_like(r[name])
            r[name][0] = jnp.where(even_row, *value)
    else:
        r["final"][...] = y[...].reshape(32, 8, 128) + r["final_in"][...]


def outputs_kernel(co, sums, final, start_o, mean_o, held):
    matrix = permutation(False)
    for p in CELLS:
        a, h, j = p
        i_p = AT[p]
        start = final[i_p] * co[COEF[("cap", 0, p)]]
        mean = sums[i_p] * co[COEF[("alpha", 0, p)]] * (1.0 / STEPS)
        held[j, pl.ds(a * 16 + h, 8, stride=2), :] = start
        held[j, pl.ds(32 + a * 16 + h, 8, stride=2), :] = mean
    for t in range(4):
        piece = jnp.concatenate([held[j, :, t * 32 : (t + 1) * 32] for j in range(8)], axis=1)
        moved = permute(piece, matrix).reshape(4, 16, 256)
        start_o[:, :, t * 256 : (t + 1) * 256] = moved[:2]
        mean_o[:, :, t * 256 : (t + 1) * 256] = moved[2:]


def struct(*shape):
    return jax.ShapeDtypeStruct(shape, F32)


VM = pl.BlockSpec(memory_space=pltpu.VMEM)
HBM = pl.BlockSpec(memory_space=pltpu.HBM)
PARAMS = pltpu.CompilerParams(vmem_limit_bytes=VMEM_LIMIT)


def call(kernel, in_specs, outs, scratch):
    return pl.pallas_call(
        kernel,
        out_shape=outs,
        in_specs=in_specs,
        out_specs=[VM] * len(outs),
        scratch_shapes=scratch,
        compiler_params=PARAMS,
    )


CELL = struct(32, 8, 128)
WAVE = struct(HALF, 2, 8, 128)
LANES = struct(8, 128)
ROWS = struct(64, 8, 128)


def run_sweep(first, last, top, bottom, sizes, inputs, outs):
    scratch = {"fields": pltpu.VMEM((4, 256, 128), F32), "f": pltpu.VMEM((320, 128), F32)}
    kept = {name: pltpu.VMEM((32, 8, 128), F32) for name in ("sums", "squares") if name not in outs}
    if not last:
        scratch["edges"] = pltpu.VMEM((2, top - bottom + 1, 2, 8, 128), F32)
        if "rows" not in outs:
            scratch["rows"] = pltpu.VMEM((2, 8, 128), F32)
    if first:
        scratch["matrix"] = pltpu.VMEM((256, 256), BF16)
        scratch["force"] = pltpu.VMEM((2, 8, 32, 128), F32)
    scratch = scratch | kept
    names = [*inputs, *outs, *scratch]
    kernel = functools.partial(sweep_kernel, first, last, top, bottom, sizes, names)
    got = call(kernel, [VM] * len(inputs), list(outs.values()), list(scratch.values()))(*inputs.values())
    return dict(zip(outs, got))


def shifts(axis):
    count = lax.axis_size(axis)
    up = [(i, (i + 1) % count) for i in range(count)]
    return up, [(j, i) for i, j in up]


def swap_all(low, high, row_low, row_high):
    up, down = shifts("cols")
    rows_up, rows_down = shifts("rows")
    return (
        lax.ppermute(high, "cols", up),
        lax.ppermute(low, "cols", down),
        lax.ppermute(row_high, "rows", rows_up),
        lax.ppermute(row_low, "rows", rows_down),
    )


def swap_pairs(near, far, axis):
    count = lax.axis_size(axis)
    near_pairs = [(i, i ^ 1) for i in range(count)]
    far_pairs = [(i, (i - 1 if i % 2 == 0 else i + 1) % count) for i in range(count)]
    got_far = lax.ppermute(far, axis, far_pairs)
    return lax.ppermute(near, axis, near_pairs), got_far


def swap_waves(waves):
    upper = swap_pairs(waves["near_upper"], waves["far_upper"], "cols")
    rows = swap_pairs(waves["row_near"], waves["row_far"], "rows")
    lower = swap_pairs(waves["near_lower"], waves["far_lower"], "cols")
    return upper, rows, lower


def later_sweep(last, sizes, n_rows, before, co, sums, waves):
    upper, rows, lower = swap_waves(waves)
    row_in = {"got_row_near": rows[0], "got_row_far": rows[1]}
    inputs = {"co": co, "sums_in": sums, "got_near": upper[0], "got_far": upper[1]} | row_in
    outs = {"y_out": struct(256, 128), "sums": CELL, "squares": CELL}
    if not last:
        outs |= {"rows": struct(2, 8, 128), "near_upper": WAVE, "far_upper": WAVE}
    mid = run_sweep(False, last, STEPS - 1, HALF, sizes, inputs, outs)
    inputs = {"co": co, "sums_in": mid["sums"], "squares_in": mid["squares"], "y_in": mid["y_out"]}
    inputs |= {"got_near": lower[0], "got_far": lower[1], "final_in": before["final"], "norms_in": before["norms"]}
    inputs |= row_in
    if last:
        outs = {"sums": CELL, "final": CELL, "norms": struct(n_rows, 1, 128)}
    else:
        inputs["rows_in"] = mid["rows"]
        outs = {"sums": CELL, "final": CELL, "norms": LANES, "near_lower": WAVE, "far_lower": WAVE}
        outs |= {"row_near": ROWS, "row_far": ROWS}
    return mid | run_sweep(False, last, HALF - 1, 0, sizes, inputs, outs)


def everywhere(x):
    x = jnp.sum(lax.all_to_all(x, "rows", 0, 0), axis=0)
    x = jnp.broadcast_to(x[None], (lax.axis_size("cols"),) + x.shape)
    return jnp.sum(lax.all_to_all(x, "cols", 0, 0), axis=0)


def local(forcing, material, capacity_table, conductance_table, sink_table):
    steps = forcing.shape[0]
    n_cols, n_rows = lax.axis_size("cols"), lax.axis_size("rows")
    sizes = (16 * n_cols, 1024 * n_rows)
    cap, con, sink, *facing = call(
        materials_kernel,
        [HBM] * 2,
        [CELL, struct(256, 128), CELL] + [struct(2, 8, 128)] * 2 + [struct(4, 8, 128)] * 2,
        [pltpu.VMEM((8, 32, 128), F32)]
        + [pltpu.SMEM((3, 8), F32), pltpu.VMEM(material.shape, jnp.int32), pltpu.SemaphoreType.DMA((2,))],
    )(jnp.stack([capacity_table, conductance_table, sink_table]), material)
    con_low, con_high, row_low, row_high = swap_all(*facing)
    column = lax.axis_index("cols") * 16 + jnp.arange(16, dtype=jnp.int32)
    row = lax.axis_index("rows") * 1024 + jnp.arange(1024, dtype=jnp.int32)
    power = column.astype(F32)[:, None] / float(sizes[0]) + row.astype(F32)[None, :] / float(sizes[1])
    source = forcing * jnp.power(jnp.float32(3.0), power)
    inputs = {"cap": cap, "con": con, "sink": sink, "con_low": con_low, "con_high": con_high}
    inputs |= {"row_low": row_low, "row_high": row_high, "forcing": source}
    outs = {"co": struct(len(KEYS), 8, 128), "sums": CELL, "final": CELL, "norms": LANES}
    outs |= {name: WAVE for name in ("near_upper", "far_upper", "near_lower", "far_lower")}
    outs |= {"row_near": ROWS, "row_far": ROWS}
    one = run_sweep(True, False, STEPS - 1, 0, sizes, inputs, outs)
    two = later_sweep(False, sizes, n_rows, one, one["co"], one["sums"], one)
    three = later_sweep(True, sizes, n_rows, two, one["co"], two["sums"], two)
    whole = struct(2, 16, 1024)
    start, mean = call(outputs_kernel, [VM] * 3, [whole, whole], [pltpu.VMEM((8, 64, 128), F32)])(
        one["co"], three["sums"], three["final"]
    )
    summed = everywhere(three["norms"])[0, :SWEEPS]
    count = float(steps * 2 * sizes[0] * sizes[1])
    return start, mean, jnp.sqrt(summed / count + 1e-06)


def solution(mesh):
    return jax.shard_map(
        local,
        mesh=mesh,
        in_specs=(P(None, None, "cols", "rows"), P(None, "cols", "rows"), P(), P(), P()),
        out_specs=(P(None, "cols", "rows"), P(None, "cols", "rows"), P()),
        check_vma=False,
    )
```
